32 devices in a mesh: seq: 16 (over z, y, x), fsdp: 1, dp: 2 (over core).
Axes of the slice: x: 2, y: 2, z: 4, core: 2. Of those that a mesh axis runs over, the one named last changes fastest.
Arguments:
- query_rows: bfloat16 [1, 2048, 2048], P('fsdp', 'seq', 'dp'), may hold values from -32 to 32
- key_rows: bfloat16 [1, 2048, 2048], P('fsdp', 'seq', 'dp'), may hold values from -32 to 32
- value_rows: bfloat16 [1, 2048, 2048], P('fsdp', 'seq', 'dp'), may hold values from -6 to 6
- summary_keys: bfloat16 [1, 128, 2048], P('fsdp', 'seq', 'dp'), may hold values from -6 to 6
- summary_values: bfloat16 [1, 128, 2048], P('fsdp', 'seq', 'dp'), may hold values from -6 to 6
- out_grad: bfloat16 [1, 2048, 2048], P('fsdp', 'seq', 'dp'), may hold values from -6 to 6
- rel_bias: float32 [4, 16], P(None, 'fsdp'), may hold values from -2 to 2
- pattern: int32 [1, 16, 3], P('fsdp'), may hold values from -1 to 15, as said below
- block_view: int32 [1, 16], P('fsdp'), may hold values from 0 to 95, as said below
- summary_view: int32 [1, 128], P('fsdp'), may hold values from 0 to 95
Outputs:
- attended: bfloat16 [1, 2048, 2048], P('fsdp', 'seq', 'dp')
- query_grad: bfloat16 [1, 2048, 2048], P('fsdp', 'seq', 'dp')
- key_grad: bfloat16 [1, 2048, 2048], P('fsdp', 'seq', 'dp')
- value_grad: bfloat16 [1, 2048, 2048], P('fsdp', 'seq', 'dp')
- summary_key_grad: bfloat16 [1, 128, 2048], P('fsdp', 'seq', 'dp')
- summary_value_grad: bfloat16 [1, 128, 2048], P('fsdp', 'seq', 'dp')
- bias_grad: float32 [4, 16], P(None, 'fsdp')
The draws below stay inside these ranges and needn't reach their ends.
Inputs may be any that keep to these rules, and one draw needn't show every extreme that they name: `pattern`: slot j of block b's list holds b + j - 1 or -1 (no block); slot 1 always holds b. `block_view`: blocks that follow each other have equal views or views one apart on the cycle of 96 views.
All inputs are finite; a program needn't handle non-finite values.
Results may differ from the reference program's by a relative error of at most 0.0074.
Values may be sent and summed in bfloat16 or wider, within the bound.
A program may use at most 64 MiB of HBM per device.

```python
import functools
import math
import jax
import jax.numpy as jnp
from jax import lax

HEADS = 16
HSIZE = 128
BLK = 128
NVIEW = 96
NREL = 4
SAMPLES = 1
TOKENS = 2048
NBLK = 16
SUMS = 128


def paired_fields(base_key):
    mixed_key = jax.random.fold_in(base_key, 11)
    first_key, second_key = jax.random.split(mixed_key, 2)
    field_shape = (SAMPLES, TOKENS, HEADS * HSIZE)
    query_draw = jnp.clip(jax.random.normal(first_key, field_shape, jnp.float32), -6.0, 6.0)
    key_draw = jnp.clip(jax.random.normal(second_key, field_shape, jnp.float32), -6.0, 6.0)
    return (query_draw, key_draw)


def draw_query_rows(key, part):
    return paired_fields(key)[0].astype(jnp.bfloat16)


def draw_key_rows(key, part):
    return paired_fields(key)[1].astype(jnp.bfloat16)


def draw_pattern(key, part):
    keeping = jax.random.randint(jax.random.fold_in(key, 37), (SAMPLES, NBLK, 3), 0, 5) < 3
    slot_ids = jnp.arange(3, dtype=jnp.int32)[None, None, :]
    blocks = jnp.arange(NBLK, dtype=jnp.int32)[None, :, None] + slot_ids - 1
    inside = (blocks >= 0) & (blocks < NBLK)
    keeping = keeping | (slot_ids == 1)
    return jnp.where(keeping & inside, blocks, -1).astype(jnp.int32)


def draw_block_view(key, part):
    first_key, second_key = jax.random.split(jax.random.fold_in(key, 23))
    start_view = jax.random.randint(first_key, (SAMPLES, 1), 0, NVIEW)
    advances = jax.random.randint(second_key, (SAMPLES, NBLK), 0, 2)
    start_view = start_view.at[0, 0].set(NVIEW - 1)
    advances = advances.at[0, 0].set(0).at[0, 1].set(1)
    return ((start_view + jnp.cumsum(advances, axis=1)) % NVIEW).astype(jnp.int32)


def set_ends(result, own_key, smallest, top_value):
    spot = [jax.random.randint(jax.random.fold_in(own_key, axis), (), 0, length) for axis, length in enumerate(result.shape)]
    widest = result.shape.index(max(result.shape))
    next_to = spot[:widest] + [(spot[widest] + 1) % result.shape[widest]] + spot[widest + 1:]
    return result.at[tuple(spot)].set(smallest).at[tuple(next_to)].set(top_value)


def shard_levels(stream_key, dims, pieces, smallest, high):
    gain, own = 1.0, jax.random.fold_in(stream_key, 6)
    for axis_at, blocks in pieces:
        steps = jnp.exp(jax.random.uniform(jax.random.fold_in(own, axis_at), (blocks,), jnp.float32, smallest / len(pieces), high / len(pieces)))
        gain = gain * jnp.repeat(steps, dims[axis_at] // blocks).reshape([-1 if axis == axis_at else 1 for axis in range(len(dims))])
    return gain


def centred(stream_key, shape, scale, most, cuts=(), held_as=jnp.bfloat16):
    entries = jax.random.normal(stream_key, shape, jnp.float32) * scale
    if len(cuts) > 0:
        entries = shard_levels(stream_key, shape, cuts, -0.22, 0.18) * entries
    return jnp.clip(entries, min=-most, max=most).astype(held_as)


def setup_inputs(seed: int = 0) -> dict:
    arg_keys = jax.random.split(jax.random.key(seed), 11)
    query_rows = draw_query_rows(jax.random.fold_in(arg_keys[10], 71), 0)
    key_rows = draw_key_rows(jax.random.fold_in(arg_keys[10], 71), 0)
    value_rows = centred(arg_keys[2], (SAMPLES, TOKENS, HEADS * HSIZE), 1.0, 6.0, ((1, 16), (2, 2)))
    summary_keys = centred(arg_keys[3], (SAMPLES, SUMS, HEADS * HSIZE), 1.0, 6.0, ((1, 16), (2, 2)))
    summary_values = centred(arg_keys[4], (SAMPLES, SUMS, HEADS * HSIZE), 1.0, 6.0, ((1, 16), (2, 2)))
    out_grad = centred(arg_keys[5], (SAMPLES, TOKENS, HEADS * HSIZE), 1.0, 6.0, ((1, 16), (2, 2)))
    rel_bias = jnp.clip(jax.random.uniform(arg_keys[6], (NREL, HEADS), jnp.float32, -2.0, 2.0), -2.0, 2.0)
    pattern = draw_pattern(jax.random.fold_in(arg_keys[10], 71), 0)
    block_view = draw_block_view(jax.random.fold_in(arg_keys[10], 71), 0)
    summary_view = set_ends(jax.random.randint(arg_keys[9], (SAMPLES, SUMS), 0, NVIEW), jax.random.fold_in(arg_keys[9], 1), 0, NVIEW - 1).astype(jnp.int32)
    return dict(query_rows=query_rows, key_rows=key_rows, value_rows=value_rows, summary_keys=summary_keys, summary_values=summary_values, out_grad=out_grad, rel_bias=rel_bias, pattern=pattern, block_view=block_view, summary_view=summary_view)


NEG_FILL = -1e+30
HIGH = lax.Precision.HIGHEST

def cycle_class(view_a, view_b):
    distance = jnp.abs(view_a - view_b)
    distance = jnp.minimum(distance, NVIEW - distance)
    return (distance >= 1).astype(jnp.int32) + (distance >= 2).astype(jnp.int32) + (distance >= 8).astype(jnp.int32)

def weighted_sum(weights, win_side, sum_side, split_at):
    first_part = jnp.einsum('nhqk,nkhd->nqhd', weights[..., :split_at].astype(jnp.float32), win_side.astype(jnp.float32), precision=HIGH)
    second_part = jnp.einsum('nhqk,khd->nqhd', weights[..., split_at:].astype(jnp.float32), sum_side.astype(jnp.float32), precision=HIGH)
    return first_part + second_part

def pair_products(left_rows, win_side, sum_side):
    first_part = jnp.einsum('nqhd,nkhd->nhqk', left_rows.astype(jnp.float32), win_side.astype(jnp.float32), precision=HIGH)
    second_part = jnp.einsum('nqhd,khd->nhqk', left_rows.astype(jnp.float32), sum_side.astype(jnp.float32), precision=HIGH)
    return jnp.concatenate([first_part, second_part], axis=3)

def one_sample(sample_items, bias_table):
    query_rows, key_rows, value_rows, summary_keys, summary_values, out_grad, pattern, block_view, summary_view = sample_items
    block_shape = (NBLK, BLK, HEADS, HSIZE)
    split_at = 3 * BLK
    score_scale = 1.0 / math.sqrt(HSIZE)
    queries = query_rows.reshape(block_shape)
    grads_out = out_grad.reshape(block_shape)
    zero_block = jnp.zeros((1, BLK, HEADS, HSIZE), key_rows.dtype)

    def windows(blocks):
        padded = jnp.concatenate([zero_block, blocks, zero_block], axis=0)
        return jnp.concatenate([padded[:-2], padded[1:-1], padded[2:]], axis=1)
    keys_win = windows(key_rows.reshape(block_shape))
    values_win = windows(value_rows.reshape(block_shape))
    keys_sum = summary_keys.reshape(SUMS, HEADS, HSIZE)
    values_sum = summary_values.reshape(SUMS, HEADS, HSIZE)
    padded_views = jnp.pad(block_view, 1)
    near_views = jnp.stack([padded_views[:-2], padded_views[1:-1], padded_views[2:]], axis=1)
    classes = jnp.concatenate([jnp.repeat(cycle_class(block_view[:, None], near_views), BLK, axis=1), cycle_class(block_view[:, None], summary_view[None, :])], axis=1)
    onehot = (classes[:, :, None] == jnp.arange(NREL, dtype=jnp.int32)[None, None, :]).astype(jnp.float32)
    bias = jnp.einsum('nkc,ch->nhk', onehot, bias_table, precision=HIGH)[:, :, None, :]
    allowed = jnp.concatenate([jnp.repeat(pattern >= 0, BLK, axis=1), jnp.ones((NBLK, SUMS), dtype=bool)], axis=1)
    scores = pair_products(queries, keys_win, keys_sum) * score_scale + bias
    scores = jnp.where(allowed[:, None, None, :], scores, NEG_FILL)
    row_max = lax.optimization_barrier(jnp.max(scores, axis=3, keepdims=True))
    lifted = jnp.exp(scores - row_max)
    row_total = lax.optimization_barrier(jnp.sum(lifted, axis=3, keepdims=True))
    weights = lifted / row_total
    weights_low = weights.astype(jnp.bfloat16)
    attended = weighted_sum(weights_low, values_win, values_sum, split_at).astype(jnp.bfloat16)
    prob_grad = pair_products(grads_out, values_win, values_sum)
    row_delta = lax.optimization_barrier(jnp.sum(weights * prob_grad, axis=3, keepdims=True))
    score_grad = weights * (prob_grad - row_delta)
    grad_low = score_grad.astype(jnp.bfloat16)
    query_grad = (weighted_sum(grad_low, keys_win, keys_sum, split_at) * score_scale).astype(jnp.bfloat16)
    win_key = jnp.einsum('nhqk,nqhd->nkhd', grad_low[..., :split_at].astype(jnp.float32), queries.astype(jnp.float32), precision=HIGH)
    win_value = jnp.einsum('nhqk,nqhd->nkhd', weights_low[..., :split_at].astype(jnp.float32), grads_out.astype(jnp.float32), precision=HIGH)
    zero_wide = jnp.zeros((1, BLK, HEADS, HSIZE), jnp.float32)

    def fold_window(window_grad):
        slots = window_grad.reshape(NBLK, 3, BLK, HEADS, HSIZE)
        return slots[:, 1] + jnp.concatenate([slots[1:, 0], zero_wide], axis=0) + jnp.concatenate([zero_wide, slots[:-1, 2]], axis=0)
    key_grad = (fold_window(win_key) * score_scale).astype(jnp.bfloat16)
    value_grad = fold_window(win_value).astype(jnp.bfloat16)
    summary_key_grad = (jnp.einsum('nhqk,nqhd->khd', grad_low[..., split_at:].astype(jnp.float32), queries.astype(jnp.float32), precision=HIGH) * score_scale).astype(jnp.bfloat16)
    summary_value_grad = jnp.einsum('nhqk,nqhd->khd', weights_low[..., split_at:].astype(jnp.float32), grads_out.astype(jnp.float32), precision=HIGH).astype(jnp.bfloat16)
    bias_term = jnp.einsum('nhqk,nkc->ch', score_grad, onehot, precision=HIGH)
    width = HEADS * HSIZE
    return (attended.reshape(TOKENS, width), query_grad.reshape(TOKENS, width), key_grad.reshape(TOKENS, width), value_grad.reshape(TOKENS, width), summary_key_grad.reshape(SUMS, width), summary_value_grad.reshape(SUMS, width), bias_term)

def reference(query_rows, key_rows, value_rows, summary_keys, summary_values, out_grad, rel_bias, pattern, block_view, summary_view):
    results = lax.map(functools.partial(one_sample, bias_table=rel_bias), (query_rows, key_rows, value_rows, summary_keys, summary_values, out_grad, pattern, block_view, summary_view))
    return (results[0], results[1], results[2], results[3], results[4], results[5], lax.optimization_barrier(jnp.sum(results[6], axis=0)))
```

```python
import functools
import math

import jax
import jax.numpy as jnp
from jax import lax
from jax.experimental import pallas as pl
from jax.experimental.pallas import tpu as pltpu
from jax.sharding import PartitionSpec as P

HSIZE = 128
BLK = 128
NVIEW = 96
NREL = 4
NEG_FILL = -1e30
F32 = jnp.float32
BF16 = jnp.bfloat16


def cycle_class(view_a, view_b):
    distance = jnp.abs(view_a - view_b)
    distance = jnp.minimum(distance, NVIEW - distance)
    return (
        (distance >= 1).astype(jnp.int32)
        + (distance >= 2).astype(jnp.int32)
        + (distance >= 8).astype(jnp.int32)
    )


def dot_nt(a, b):
    return lax.dot_general(a, b, (((1,), (1,)), ((), ())), preferred_element_type=F32)


def dot_nn(a, b):
    return lax.dot_general(a, b, (((1,), (0,)), ((), ())), preferred_element_type=F32)


def dot_tn(a, b):
    return lax.dot_general(a, b, (((0,), (0,)), ((), ())), preferred_element_type=F32)


def kernel(
    sizes,
    q_ref, k_ref, v_ref, sk_ref, sv_ref, do_ref, tab_ref, pat_ref, bv_ref, view_ref,
    att_ref, dq_ref, dk_ref, dv_ref, dsk_ref, dsv_ref, db_ref,
    kx, vx, qg, dog, sum_out, sum_in, ksm, vsm, dkx, dvx, dks, dvs,
    stage, halo_out, halo_in, rs_out, rs_in, b_out, b_in, x_in,
    in_send, in_recv, kv_send, kv_recv, sum_send, sum_recv, out_send, out_recv,
    hg_send, hg_recv, rs_send, rs_recv, b_send, b_recv, x_send, x_recv,
):
    S, D, G, T, W, HG, SR = sizes
    planes = S // G
    WG = HG * HSIZE
    H = G * HG
    blocks_dev = T // BLK
    nblk = G * blocks_dev
    total_blocks = planes * nblk
    scale = 1.0 / math.sqrt(HSIZE)
    brows = b_out.shape[0]

    s = lax.axis_index("seq")
    dp = lax.axis_index("dp")
    plane = s // G
    lane = lax.rem(s, G)
    first = plane * G

    def remote(src, dst, send, recv, target):
        return pltpu.make_async_remote_copy(
            src_ref=src, dst_ref=dst, send_sem=send, recv_sem=recv,
            device_id=target, device_id_type=pl.DeviceIdType.MESH,
        )

    def landed(dst, sem):
        pltpu.make_async_copy(dst, dst, sem).wait()

    barrier = pltpu.get_barrier_semaphore()
    for d in range(1, S):
        pl.semaphore_signal(
            barrier, inc=1, device_id={"seq": lax.rem(s + d, S)},
            device_id_type=pl.DeviceIdType.MESH,
        )
    for d in range(1, D):
        pl.semaphore_signal(
            barrier, inc=1, device_id={"dp": lax.rem(dp + d, D)},
            device_id_type=pl.DeviceIdType.MESH,
        )
    sum_out[...] = jnp.concatenate(
        [sk_ref[0].astype(F32), sv_ref[0].astype(F32)], axis=0
    ).astype(BF16)
    pl.semaphore_wait(barrier, S - 1 + D - 1)

    def cols(index):
        return pl.ds(pl.multiple_of(index * WG, WG), WG)

    def rows_at(index, base):
        return pl.ds(pl.multiple_of(base + index * T, BLK), T)

    sends = []
    pairs = ((k_ref, kx, BLK), (v_ref, vx, BLK), (q_ref, qg, 0), (do_ref, dog, 0))

    def send_pairs(which):
        for a in which:
            src, dst, base = pairs[a]
            for d in range(1, G):
                to = lax.rem(lane + d, G)
                copy = remote(
                    src.at[0, :, cols(to)], dst.at[rows_at(lane, base), :],
                    in_send.at[a, d], in_recv.at[a, lane], {"seq": first + to},
                )
                copy.start()
                sends.append(copy)
            pltpu.make_async_copy(
                src.at[0, :, cols(lane)], dst.at[rows_at(lane, base), :], in_recv.at[a, lane]
            ).start()

    send_pairs((0, 1))
    for d in range(1, S):
        to = lax.rem(s + d, S)
        copy = remote(
            sum_out.at[:, cols(lax.rem(to, G))], sum_in.at[s],
            sum_send.at[d], sum_recv.at[s], {"seq": to},
        )
        copy.start()
        sends.append(copy)
    pltpu.make_async_copy(sum_out.at[:, cols(lane)], sum_in.at[s], sum_recv.at[s]).start()
    send_pairs((2, 3))

    dkx[...] = jnp.zeros_like(dkx)
    dvx[...] = jnp.zeros_like(dvx)
    dks[...] = jnp.zeros_like(dks)
    dvs[...] = jnp.zeros_like(dvs)

    has_prev = plane > 0
    has_next = plane < planes - 1
    top = (G * T, G * T + BLK)
    low = (BLK, 2 * BLK)
    last = (BLK + G * T, 2 * BLK + G * T)

    for a in range(2):
        for j in range(G):
            landed(pairs[a][1].at[pl.ds(BLK + j * T, T), :], in_recv.at[a, j])

    def halo_copy(a, forward):
        buf = (kx, vx)[a]
        if forward:
            return remote(
                buf.at[pl.ds(top[0], BLK), :], buf.at[pl.ds(0, BLK), :],
                kv_send.at[0, a], kv_recv.at[0, a], {"seq": lax.rem(s + G, S)},
            )
        return remote(
            buf.at[pl.ds(low[0], BLK), :], buf.at[pl.ds(last[0], BLK), :],
            kv_send.at[1, a], kv_recv.at[1, a], {"seq": lax.rem(s + S - G, S)},
        )

    @pl.when(has_next)
    def _():
        for a in range(2):
            halo_copy(a, True).start()

    @pl.when(has_prev)
    def _():
        for a in range(2):
            halo_copy(a, False).start()

    @pl.when(jnp.logical_not(has_prev))
    def _():
        for buf in (kx, vx):
            buf[0:BLK, :] = jnp.zeros((BLK, WG), BF16)

    @pl.when(jnp.logical_not(has_next))
    def _():
        for buf in (kx, vx):
            buf[last[0]:last[1], :] = jnp.zeros((BLK, WG), BF16)

    for j in range(S):
        landed(sum_in.at[j], sum_recv.at[j])
    both = sum_in[...].astype(F32)
    ksm[...] = both[:, :SR, :].reshape(S * SR, WG).astype(BF16)
    vsm[...] = both[:, SR:, :].reshape(S * SR, WG).astype(BF16)
    view_rows = jnp.broadcast_to(view_ref[...].astype(F32), (BLK, S * SR)).T.astype(jnp.int32)

    for a in (2, 3):
        for j in range(G):
            landed(pairs[a][1].at[pl.ds(j * T, T), :], in_recv.at[a, j])

    @pl.when(has_prev)
    def _():
        for a in range(2):
            landed((kx, vx)[a].at[pl.ds(0, BLK), :], kv_recv.at[0, a])

    @pl.when(has_next)
    def _():
        for a in range(2):
            landed((kx, vx)[a].at[pl.ds(last[0], BLK), :], kv_recv.at[1, a])

    bias_acc = [jnp.zeros((1, BLK), F32) for _ in range(HG * NREL)]

    def one_block(n):
        block = plane * nblk + n
        view = bv_ref[0, block]
        slot_class = []
        slot_open = []
        for j in range(3):
            near = jnp.clip(block + (j - 1), 0, total_blocks - 1)
            slot_class.append(cycle_class(view, bv_ref[0, near]))
            slot_open.append(pat_ref[0, block, j] >= 0)
        sum_class = cycle_class(view, view_rows)
        here = slice(n * BLK, (n + 1) * BLK)
        win = slice(n * BLK, (n + 3) * BLK)
        for h in range(HG):
            hc = slice(h * HSIZE, (h + 1) * HSIZE)
            head = dp * H + lane * HG + h
            table = [tab_ref[c, head] for c in range(NREL)]
            q = qg[here, hc]
            do = dog[here, hc]
            kw = kx[win, hc]
            vw = vx[win, hc]
            ks = ksm[:, hc]
            vs = vsm[:, hc]
            raw = dot_nt(kw, q)
            scores = []
            for j in range(3):
                c = slot_class[j]
                b = jnp.where(
                    c >= 2, jnp.where(c == 3, table[3], table[2]),
                    jnp.where(c == 1, table[1], table[0]),
                )
                b = jnp.where(slot_open[j], b, NEG_FILL)
                scores.append(raw[j * BLK:(j + 1) * BLK] * scale + b)
            sum_bias = jnp.where(
                sum_class >= 2, jnp.where(sum_class == 3, table[3], table[2]),
                jnp.where(sum_class == 1, table[1], table[0]),
            )
            scores.append(dot_nt(ks, q) * scale + sum_bias)
            top_score = functools.reduce(
                jnp.maximum, [jnp.max(x, axis=0, keepdims=True) for x in scores]
            )
            lifted = [jnp.exp(x - top_score) for x in scores]
            total = sum(jnp.sum(x, axis=0, keepdims=True) for x in lifted)
            inverse = 1.0 / total
            weights = [x * inverse for x in lifted]
            dpw = dot_nt(vw, do)
            prob = [dpw[j * BLK:(j + 1) * BLK] for j in range(3)] + [dot_nt(vs, do)]
            delta = sum(jnp.sum(w * x, axis=0, keepdims=True) for w, x in zip(weights, prob))
            grads = [w * (x - delta) for w, x in zip(weights, prob)]
            w_win = jnp.concatenate([w.astype(BF16) for w in weights[:3]], axis=0)
            w_sum = weights[3].astype(BF16)
            g_win = jnp.concatenate([g.astype(BF16) for g in grads[:3]], axis=0)
            g_sum = grads[3].astype(BF16)
            stage[0, here, hc] = (dot_tn(w_win, vw) + dot_tn(w_sum, vs)).astype(BF16)
            stage[1, here, hc] = ((dot_tn(g_win, kw) + dot_tn(g_sum, ks)) * scale).astype(BF16)
            dkx[win, hc] += dot_nn(g_win, q)
            dvx[win, hc] += dot_nn(w_win, do)
            dks[:, hc] += dot_nn(g_sum, q)
            dvs[:, hc] += dot_nn(w_sum, do)
            slot_sums = [jnp.sum(g, axis=0, keepdims=True) for g in grads[:3]]
            for c in range(NREL):
                term = jnp.sum(jnp.where(sum_class == c, grads[3], 0.0), axis=0, keepdims=True)
                for j in range(3):
                    term = term + slot_sums[j] * jnp.where(slot_class[j] == c, 1.0, 0.0)
                bias_acc[h * NREL + c] = bias_acc[h * NREL + c] + term

    outs = (att_ref, dq_ref, dk_ref, dv_ref)

    def out_copy(a, b):
        return remote(
            stage.at[a, pl.ds(b * T, T), :], outs[a].at[0, :, cols(lane)],
            out_send.at[a, b], out_recv.at[a, lane], {"seq": first + b},
        )

    def send_out(which, b):
        @pl.when(lane != b)
        def _():
            for a in which:
                out_copy(a, b).start()

        @pl.when(lane == b)
        def _():
            for a in which:
                pltpu.make_async_copy(
                    stage.at[a, pl.ds(b * T, T), :], outs[a].at[0, :, cols(lane)],
                    out_recv.at[a, lane],
                ).start()

    def halo_grad(back, a):
        i = (0 if back else 2) + a
        return remote(
            halo_out.at[i], halo_in.at[i], hg_send.at[i], hg_recv.at[i],
            {"seq": lax.rem(s + (S - G if back else G), S)},
        )

    def finish(b):
        span = slice(BLK + b * T, BLK + (b + 1) * T)
        stage[2, b * T:(b + 1) * T, :] = (dkx[span, :] * scale).astype(BF16)
        stage[3, b * T:(b + 1) * T, :] = dvx[span, :].astype(BF16)
        send_out((2, 3), b)

    order = list(dict.fromkeys([0, G - 1] + list(range(1, G - 1))))
    for b in order:
        for i in range(blocks_dev):
            one_block(b * blocks_dev + i)
        send_out((0, 1), b)
        if b == 0:
            halo_out[0] = dkx[0:BLK, :].astype(BF16)
            halo_out[1] = dvx[0:BLK, :].astype(BF16)

            @pl.when(has_prev)
            def _():
                for a in range(2):
                    halo_grad(True, a).start()
        if b == G - 1:
            halo_out[2] = dkx[last[0]:last[1], :].astype(BF16)
            halo_out[3] = dvx[last[0]:last[1], :].astype(BF16)

            @pl.when(has_next)
            def _():
                for a in range(2):
                    halo_grad(False, a).start()

    for b in range(1, G - 1):
        finish(b)

    packed = jnp.concatenate(
        [(dks[...] * scale).reshape(S, SR, WG), dvs[...].reshape(S, SR, WG)], axis=1
    )
    rs_out[...] = packed.astype(BF16)
    pad = brows - HG * NREL
    b_out[...] = jnp.concatenate(
        bias_acc + ([jnp.zeros((pad, BLK), F32)] if pad else []), axis=0
    )
    for d in range(1, S):
        to = lax.rem(s + d, S)
        copy = remote(b_out, b_in.at[s], b_send.at[d], b_recv.at[s], {"seq": to})
        copy.start()
        sends.append(copy)
        copy = remote(rs_out.at[to], rs_in.at[s], rs_send.at[d], rs_recv.at[s], {"seq": to})
        copy.start()
        sends.append(copy)
    pltpu.make_async_copy(b_out, b_in.at[s], b_recv.at[s]).start()
    pltpu.make_async_copy(rs_out.at[s], rs_in.at[s], rs_recv.at[s]).start()

    @pl.when(has_prev)
    def _():
        for a, buf in enumerate((dkx, dvx)):
            landed(halo_in.at[2 + a], hg_recv.at[2 + a])
            buf[low[0]:low[1], :] += halo_in[2 + a].astype(F32)

    @pl.when(has_next)
    def _():
        for a, buf in enumerate((dkx, dvx)):
            landed(halo_in.at[a], hg_recv.at[a])
            buf[top[0]:top[1], :] += halo_in[a].astype(F32)

    for b in sorted({0, G - 1}):
        finish(b)

    for j in range(S):
        landed(b_in.at[j], b_recv.at[j])
    x_in[dp] = jnp.sum(b_in[...].reshape(planes, G, brows, BLK), axis=0)
    for d in range(1, D):
        copy = remote(
            x_in.at[dp], x_in.at[dp], x_send.at[d], x_recv.at[dp], {"dp": lax.rem(dp + d, D)}
        )
        copy.start()
        sends.append(copy)

    for j in range(S):
        landed(rs_in.at[j], rs_recv.at[j])
    terms = jnp.sum(rs_in[...].astype(F32).reshape(planes, G, 2 * SR, WG), axis=0)
    for g in range(G):
        gc = slice(g * WG, (g + 1) * WG)
        dsk_ref[0, :, gc] = terms[g, :SR].astype(BF16)
        dsv_ref[0, :, gc] = terms[g, SR:].astype(BF16)

    for d in range(1, D):
        who = lax.rem(dp + d, D)
        landed(x_in.at[who], x_recv.at[who])
    lanes = lax.broadcasted_iota(jnp.int32, db_ref.shape, 1)
    result = jnp.zeros(db_ref.shape, F32)
    for e in range(D):
        for g in range(G):
            column = jnp.sum(x_in[e, g], axis=1, keepdims=True)
            for h in range(HG):
                at = e * H + g * HG + h
                result = jnp.where(lanes == at, column[h * NREL:(h + 1) * NREL], result)
    db_ref[...] = result

    for a in range(4):
        for j in range(G):
            landed(outs[a].at[0, :, pl.ds(j * WG, WG)], out_recv.at[a, j])

    for copy in sends:
        copy.wait_send()
    for b in range(G):
        @pl.when(lane != b)
        def _():
            for a in range(4):
                out_copy(a, b).wait_send()

    @pl.when(has_next)
    def _():
        for a in range(2):
            halo_copy(a, True).wait_send()
            halo_grad(False, a).wait_send()

    @pl.when(has_prev)
    def _():
        for a in range(2):
            halo_copy(a, False).wait_send()
            halo_grad(True, a).wait_send()


def body(
    query_rows, key_rows, value_rows, summary_keys, summary_values, out_grad,
    rel_bias, pattern, block_view, summary_view,
):
    S = lax.axis_size("seq")
    D = lax.axis_size("dp")
    F = lax.axis_size("fsdp")
    T, W = query_rows.shape[1:]
    SR = summary_keys.shape[1]
    heads = W // HSIZE
    G = next(g for g in (4, 2, 1) if S % g == 0 and heads % g == 0)
    HG = heads // G
    WG = HG * HSIZE
    brows = -(-HG * NREL // 8) * 8
    table = lax.all_gather(rel_bias, "fsdp", axis=1, tiled=True) if F > 1 else rel_bias
    rows_ext = G * T + 2 * BLK
    vmem = pl.BlockSpec(memory_space=pltpu.VMEM)
    smem = pl.BlockSpec(memory_space=pltpu.SMEM)
    dma = pltpu.SemaphoreType.DMA
    big = jax.ShapeDtypeStruct((1, T, W), BF16)
    small = jax.ShapeDtypeStruct((1, SR, W), BF16)
    results = pl.pallas_call(
        functools.partial(kernel, (S, D, G, T, W, HG, SR)),
        out_shape=(big, big, big, big, small, small, jax.ShapeDtypeStruct(table.shape, F32)),
        in_specs=[vmem] * 6 + [smem] * 3 + [vmem],
        out_specs=[vmem] * 7,
        scratch_shapes=[
            pltpu.VMEM((rows_ext, WG), BF16),
            pltpu.VMEM((rows_ext, WG), BF16),
            pltpu.VMEM((G * T, WG), BF16),
            pltpu.VMEM((G * T, WG), BF16),
            pltpu.VMEM((2 * SR, W), BF16),
            pltpu.VMEM((S, 2 * SR, WG), BF16),
            pltpu.VMEM((S * SR, WG), BF16),
            pltpu.VMEM((S * SR, WG), BF16),
            pltpu.VMEM((rows_ext, WG), F32),
            pltpu.VMEM((rows_ext, WG), F32),
            pltpu.VMEM((S * SR, WG), F32),
            pltpu.VMEM((S * SR, WG), F32),
            pltpu.VMEM((4, G * T, WG), BF16),
            pltpu.VMEM((4, BLK, WG), BF16),
            pltpu.VMEM((4, BLK, WG), BF16),
            pltpu.VMEM((S, 2 * SR, WG), BF16),
            pltpu.VMEM((S, 2 * SR, WG), BF16),
            pltpu.VMEM((brows, BLK), F32),
            pltpu.VMEM((S, brows, BLK), F32),
            pltpu.VMEM((D, G, brows, BLK), F32),
            dma((4, G)), dma((4, G)), dma((2, 2)), dma((2, 2)), dma((S,)), dma((S,)),
            dma((4, G)), dma((4, G)), dma((4,)), dma((4,)), dma((S,)), dma((S,)),
            dma((S,)), dma((S,)), dma((D,)), dma((D,)),
        ],
        compiler_params=pltpu.CompilerParams(
            collective_id=0, has_side_effects=True, vmem_limit_bytes=40 * 1024 * 1024
        ),
    )(
        query_rows, key_rows, value_rows, summary_keys, summary_values, out_grad,
        table, pattern, block_view, summary_view,
    )
    bias_grad = results[6]
    if F > 1:
        bias_total = lax.psum(bias_grad, "fsdp")
        part = table.shape[1] // F
        bias_grad = lax.dynamic_slice_in_dim(bias_total, lax.axis_index("fsdp") * part, part, 1)
    return (*results[:6], bias_grad)


def solution(mesh):
    rows = P("fsdp", "seq", "dp")
    placed = (
        rows, rows, rows, rows, rows, rows,
        P(None, "fsdp"), P("fsdp", None, None), P("fsdp", None), P("fsdp", None),
    )
    return jax.shard_map(
        body, mesh=mesh, in_specs=placed,
        out_specs=(rows, rows, rows, rows, rows, rows, P(None, "fsdp")),
        check_vma=False,
    )
```

```python
import functools
import math

import jax
import jax.numpy as jnp
from jax import lax
from jax.experimental import pallas as pl
from jax.experimental.pallas import tpu as pltpu
from jax.sharding import PartitionSpec as P

HSIZE = 128
BLK = 128
NVIEW = 96
NREL = 4
NEG_FILL = -1e30
LIMIT = 60 * 1024 * 1024
F32 = jnp.float32
BF16 = jnp.bfloat16


def cycle_class(view_a, view_b):
    distance = jnp.abs(view_a - view_b)
    distance = jnp.minimum(distance, NVIEW - distance)
    return (
        (distance >= 1).astype(jnp.int32)
        + (distance >= 2).astype(jnp.int32)
        + (distance >= 8).astype(jnp.int32)
    )


def dot_nt(a, b):
    return lax.dot_general(a, b, (((1,), (1,)), ((), ())), preferred_element_type=F32)


def dot_nn(a, b):
    return lax.dot_general(a, b, (((1,), (0,)), ((), ())), preferred_element_type=F32)


def dot_tn(a, b):
    return lax.dot_general(a, b, (((0,), (0,)), ((), ())), preferred_element_type=F32)


def kernel(
    sizes,
    q_ref, k_ref, v_ref, sum_out, do_ref, tab_ref, pat_ref, bv_ref, view_ref,
    att_ref, dq_ref, dk_ref, dv_ref, dsum_ref, db_ref,
    kx, vx, qg, dog, sum_in, ksm, vsm, dkx, dvx, dks, dvs,
    stage, halo_out, halo_in, rs_out, rs_in, b_out, b_in, x_in,
    in_send, in_recv, kv_send, kv_recv, sum_send, sum_recv, out_send, out_recv,
    hg_send, hg_recv, rs_send, rs_recv, b_send, b_recv, x_send, x_recv,
):
    S, D, G, T, W, HG, SR = sizes
    planes = S // G
    WG = HG * HSIZE
    H = G * HG
    blocks_dev = T // BLK
    nblk = G * blocks_dev
    total_blocks = planes * nblk
    scale = 1.0 / math.sqrt(HSIZE)
    brows = b_out.shape[0]

    s = lax.axis_index("seq")
    dp = lax.axis_index("dp")
    plane = s // G
    lane = lax.rem(s, G)
    first = plane * G

    def remote(src, dst, send, recv, target):
        return pltpu.make_async_remote_copy(
            src_ref=src, dst_ref=dst, send_sem=send, recv_sem=recv,
            device_id=target, device_id_type=pl.DeviceIdType.MESH,
        )

    def landed(dst, sem):
        pltpu.make_async_copy(dst, dst, sem).wait()

    barrier = pltpu.get_barrier_semaphore()
    for d in range(1, S):
        pl.semaphore_signal(
            barrier, inc=1, device_id={"seq": lax.rem(s + d, S)},
            device_id_type=pl.DeviceIdType.MESH,
        )
    for d in range(1, D):
        pl.semaphore_signal(
            barrier, inc=1, device_id={"dp": lax.rem(dp + d, D)},
            device_id_type=pl.DeviceIdType.MESH,
        )
    pl.semaphore_wait(barrier, S - 1 + D - 1)

    def cols(index):
        return pl.ds(pl.multiple_of(index * WG, WG), WG)

    def head_cols(index, h):
        return pl.ds(pl.multiple_of(index * WG + h * HSIZE, HSIZE), HSIZE)

    def rows_at(index, base):
        return pl.ds(pl.multiple_of(base + index * T, BLK), T)

    sends = []
    pairs = ((k_ref, kx, BLK), (v_ref, vx, BLK), (q_ref, qg, 0), (do_ref, dog, 0))

    def send_pairs(which, h):
        hc = pl.ds(h * HSIZE, HSIZE)
        for a in which:
            src, dst, base = pairs[a]
            for d in range(1, G):
                to = lax.rem(lane + d, G)
                copy = remote(
                    src.at[0, :, head_cols(to, h)], dst.at[rows_at(lane, base), hc],
                    in_send.at[a, h, d], in_recv.at[a, h, lane], {"seq": first + to},
                )
                copy.start()
                sends.append(copy)
            pltpu.make_async_copy(
                src.at[0, :, head_cols(lane, h)], dst.at[rows_at(lane, base), hc],
                in_recv.at[a, h, lane],
            ).start()

    send_pairs((0, 1), 0)
    for d in range(1, S):
        to = lax.rem(s + d, S)
        copy = remote(
            sum_out.at[0, :, cols(lax.rem(to, G))], sum_in.at[s],
            sum_send.at[d], sum_recv.at[s], {"seq": to},
        )
        copy.start()
        sends.append(copy)
    pltpu.make_async_copy(sum_out.at[0, :, cols(lane)], sum_in.at[s], sum_recv.at[s]).start()
    send_pairs((2, 3), 0)
    for h in range(1, HG):
        send_pairs((0, 1, 2, 3), h)

    dkx[...] = jnp.zeros_like(dkx)
    dvx[...] = jnp.zeros_like(dvx)
    dks[...] = jnp.zeros_like(dks)
    dvs[...] = jnp.zeros_like(dvs)

    has_prev = plane > 0
    has_next = plane < planes - 1
    top = (G * T, G * T + BLK)
    low = (BLK, 2 * BLK)
    last = (BLK + G * T, 2 * BLK + G * T)

    @pl.when(jnp.logical_not(has_prev))
    def _():
        for buf in (kx, vx):
            buf[0:BLK, :] = jnp.zeros((BLK, WG), BF16)

    @pl.when(jnp.logical_not(has_next))
    def _():
        for buf in (kx, vx):
            buf[last[0]:last[1], :] = jnp.zeros((BLK, WG), BF16)

    def halo_copy(a, h, forward):
        buf = (kx, vx)[a]
        hc = pl.ds(h * HSIZE, HSIZE)
        if forward:
            return remote(
                buf.at[pl.ds(top[0], BLK), hc], buf.at[pl.ds(0, BLK), hc],
                kv_send.at[0, a, h], kv_recv.at[0, a, h], {"seq": lax.rem(s + G, S)},
            )
        return remote(
            buf.at[pl.ds(low[0], BLK), hc], buf.at[pl.ds(last[0], BLK), hc],
            kv_send.at[1, a, h], kv_recv.at[1, a, h], {"seq": lax.rem(s + S - G, S)},
        )

    def take_keys(h):
        for a in range(2):
            for j in range(G):
                landed(
                    pairs[a][1].at[pl.ds(BLK + j * T, T), pl.ds(h * HSIZE, HSIZE)],
                    in_recv.at[a, h, j],
                )

        @pl.when(has_next)
        def _():
            for a in range(2):
                halo_copy(a, h, True).start()

        @pl.when(has_prev)
        def _():
            for a in range(2):
                halo_copy(a, h, False).start()

    def take_rest(h):
        hc = pl.ds(h * HSIZE, HSIZE)
        for a in (2, 3):
            for j in range(G):
                landed(pairs[a][1].at[pl.ds(j * T, T), hc], in_recv.at[a, h, j])

        @pl.when(has_prev)
        def _():
            for a in range(2):
                landed((kx, vx)[a].at[pl.ds(0, BLK), hc], kv_recv.at[0, a, h])

        @pl.when(has_next)
        def _():
            for a in range(2):
                landed((kx, vx)[a].at[pl.ds(last[0], BLK), hc], kv_recv.at[1, a, h])

    take_keys(0)
    for j in range(S):
        landed(sum_in.at[j], sum_recv.at[j])
    both = sum_in[...].astype(F32)
    ksm[...] = both[:, :SR, :].reshape(S * SR, WG).astype(BF16)
    vsm[...] = both[:, SR:, :].reshape(S * SR, WG).astype(BF16)
    view_rows = jnp.broadcast_to(view_ref[...].astype(F32), (BLK, S * SR)).T.astype(jnp.int32)

    bias_acc = [jnp.zeros((1, BLK), F32) for _ in range(HG * NREL)]

    def one_block(h, n):
        block = plane * nblk + n
        view = bv_ref[0, block]
        slot_class = []
        slot_open = []
        for j in range(3):
            near = jnp.clip(block + (j - 1), 0, total_blocks - 1)
            slot_class.append(cycle_class(view, bv_ref[0, near]))
            slot_open.append(pat_ref[0, block, j] >= 0)
        sum_class = cycle_class(view, view_rows)
        here = slice(n * BLK, (n + 1) * BLK)
        win = slice(n * BLK, (n + 3) * BLK)
        if True:
            hc = slice(h * HSIZE, (h + 1) * HSIZE)
            head = dp * H + lane * HG + h
            table = [tab_ref[c, head] for c in range(NREL)]
            q = qg[here, hc]
            do = dog[here, hc]
            kw = kx[win, hc]
            vw = vx[win, hc]
            ks = ksm[:, hc]
            vs = vsm[:, hc]
            raw = dot_nt(kw, q)
            scores = []
            for j in range(3):
                c = slot_class[j]
                b = jnp.where(
                    c >= 2, jnp.where(c == 3, table[3], table[2]),
                    jnp.where(c == 1, table[1], table[0]),
                )
                b = jnp.where(slot_open[j], b, NEG_FILL)
                scores.append(raw[j * BLK:(j + 1) * BLK] * scale + b)
            sum_bias = jnp.where(
                sum_class >= 2, jnp.where(sum_class == 3, table[3], table[2]),
                jnp.where(sum_class == 1, table[1], table[0]),
            )
            scores.append(dot_nt(ks, q) * scale + sum_bias)
            top_score = functools.reduce(
                jnp.maximum, [jnp.max(x, axis=0, keepdims=True) for x in scores]
            )
            lifted = [jnp.exp(x - top_score) for x in scores]
            total = sum(jnp.sum(x, axis=0, keepdims=True) for x in lifted)
            inverse = 1.0 / total
            weights = [x * inverse for x in lifted]
            dpw = dot_nt(vw, do)
            prob = [dpw[j * BLK:(j + 1) * BLK] for j in range(3)] + [dot_nt(vs, do)]
            delta = sum(jnp.sum(w * x, axis=0, keepdims=True) for w, x in zip(weights, prob))
            grads = [w * (x - delta) for w, x in zip(weights, prob)]
            w_win = jnp.concatenate([w.astype(BF16) for w in weights[:3]], axis=0)
            w_sum = weights[3].astype(BF16)
            g_win = jnp.concatenate([g.astype(BF16) for g in grads[:3]], axis=0)
            g_sum = grads[3].astype(BF16)
            stage[0, here, hc] = (dot_tn(w_win, vw) + dot_tn(w_sum, vs)).astype(BF16)
            stage[1, here, hc] = ((dot_tn(g_win, kw) + dot_tn(g_sum, ks)) * scale).astype(BF16)
            dkx[win, hc] += dot_nn(g_win, q)
            dvx[win, hc] += dot_nn(w_win, do)
            dks[:, hc] += dot_nn(g_sum, q)
            dvs[:, hc] += dot_nn(w_sum, do)
            slot_sums = [jnp.sum(g, axis=0, keepdims=True) for g in grads[:3]]
            for c in range(NREL):
                term = jnp.sum(jnp.where(sum_class == c, grads[3], 0.0), axis=0, keepdims=True)
                for j in range(3):
                    term = term + slot_sums[j] * jnp.where(slot_class[j] == c, 1.0, 0.0)
                bias_acc[h * NREL + c] = bias_acc[h * NREL + c] + term

    outs = (att_ref, dq_ref, dk_ref, dv_ref)

    def out_parts(a, h, b):
        return (
            stage.at[a, pl.ds(b * T, T), pl.ds(h * HSIZE, HSIZE)],
            outs[a].at[0, :, head_cols(lane, h)],
        )

    def out_copy(a, h, b):
        src, dst = out_parts(a, h, b)
        return remote(
            src, dst, out_send.at[a, h, b], out_recv.at[a, h, lane], {"seq": first + b}
        )

    def send_out(which, h, b):
        @pl.when(lane != b)
        def _():
            for a in which:
                out_copy(a, h, b).start()

        @pl.when(lane == b)
        def _():
            for a in which:
                src, dst = out_parts(a, h, b)
                pltpu.make_async_copy(src, dst, out_recv.at[a, h, lane]).start()

    def halo_grad(back, a, h):
        i = (0 if back else 2) + a
        return remote(
            halo_out.at[h, i], halo_in.at[h, i], hg_send.at[h, i], hg_recv.at[h, i],
            {"seq": lax.rem(s + (S - G if back else G), S)},
        )

    def finish(h, b):
        span = slice(BLK + b * T, BLK + (b + 1) * T)
        hc = slice(h * HSIZE, (h + 1) * HSIZE)
        stage[2, b * T:(b + 1) * T, hc] = (dkx[span, hc] * scale).astype(BF16)
        stage[3, b * T:(b + 1) * T, hc] = dvx[span, hc].astype(BF16)
        send_out((2, 3), h, b)

    def finish_ends(h):
        hc = slice(h * HSIZE, (h + 1) * HSIZE)

        @pl.when(has_prev)
        def _():
            for a, buf in enumerate((dkx, dvx)):
                landed(halo_in.at[h, 2 + a], hg_recv.at[h, 2 + a])
                buf[low[0]:low[1], hc] += halo_in[h, 2 + a].astype(F32)

        @pl.when(has_next)
        def _():
            for a, buf in enumerate((dkx, dvx)):
                landed(halo_in.at[h, a], hg_recv.at[h, a])
                buf[top[0]:top[1], hc] += halo_in[h, a].astype(F32)

        for b in sorted({0, G - 1}):
            finish(h, b)

    order = list(dict.fromkeys([0, G - 1] + list(range(1, G - 1))))
    half = len(order) // 2
    for h in range(HG):
        hc = slice(h * HSIZE, (h + 1) * HSIZE)
        take_rest(h)
        for step, b in enumerate(order):
            if step == half:
                if h + 1 < HG:
                    take_keys(h + 1)
                if h > 0:
                    finish_ends(h - 1)
            for i in range(blocks_dev):
                one_block(h, b * blocks_dev + i)
            send_out((0, 1), h, b)
            if b == 0:
                halo_out[h, 0] = dkx[0:BLK, hc].astype(BF16)
                halo_out[h, 1] = dvx[0:BLK, hc].astype(BF16)

                @pl.when(has_prev)
                def _():
                    for a in range(2):
                        halo_grad(True, a, h).start()
            if b == G - 1:
                halo_out[h, 2] = dkx[last[0]:last[1], hc].astype(BF16)
                halo_out[h, 3] = dvx[last[0]:last[1], hc].astype(BF16)

                @pl.when(has_next)
                def _():
                    for a in range(2):
                        halo_grad(False, a, h).start()
        for b in range(1, G - 1):
            finish(h, b)

    packed = jnp.concatenate(
        [(dks[...] * scale).reshape(S, SR, WG), dvs[...].reshape(S, SR, WG)], axis=1
    )
    rs_out[...] = packed.astype(BF16)
    pad = brows - HG * NREL
    b_out[...] = jnp.concatenate(
        bias_acc + ([jnp.zeros((pad, BLK), F32)] if pad else []), axis=0
    )
    for d in range(1, S):
        to = lax.rem(s + d, S)
        copy = remote(b_out, b_in.at[s], b_send.at[d], b_recv.at[s], {"seq": to})
        copy.start()
        sends.append(copy)
        copy = remote(rs_out.at[to], rs_in.at[s], rs_send.at[d], rs_recv.at[s], {"seq": to})
        copy.start()
        sends.append(copy)
    pltpu.make_async_copy(b_out, b_in.at[s], b_recv.at[s]).start()
    pltpu.make_async_copy(rs_out.at[s], rs_in.at[s], rs_recv.at[s]).start()

    finish_ends(HG - 1)

    for j in range(S):
        landed(b_in.at[j], b_recv.at[j])
    x_in[dp] = jnp.sum(b_in[...].reshape(planes, G, brows, BLK), axis=0)
    for d in range(1, D):
        copy = remote(
            x_in.at[dp], x_in.at[dp], x_send.at[d], x_recv.at[dp], {"dp": lax.rem(dp + d, D)}
        )
        copy.start()
        sends.append(copy)

    for j in range(S):
        landed(rs_in.at[j], rs_recv.at[j])
    terms = jnp.sum(rs_in[...].astype(F32).reshape(planes, G, 2 * SR, WG), axis=0)
    for g in range(G):
        gc = slice(g * WG, (g + 1) * WG)
        dsum_ref[0, :, gc] = terms[g].astype(BF16)

    for d in range(1, D):
        who = lax.rem(dp + d, D)
        landed(x_in.at[who], x_recv.at[who])
    lanes = lax.broadcasted_iota(jnp.int32, db_ref.shape, 1)
    result = jnp.zeros(db_ref.shape, F32)
    for e in range(D):
        for g in range(G):
            column = jnp.sum(x_in[e, g], axis=1, keepdims=True)
            for h in range(HG):
                at = e * H + g * HG + h
                result = jnp.where(lanes == at, column[h * NREL:(h + 1) * NREL], result)
    db_ref[...] = result

    for a in range(4):
        for h in range(HG):
            for j in range(G):
                landed(
                    outs[a].at[0, :, pl.ds(j * WG + h * HSIZE, HSIZE)], out_recv.at[a, h, j]
                )

    for copy in sends:
        copy.wait_send()
    for b in range(G):
        @pl.when(lane != b)
        def _():
            for a in range(4):
                for h in range(HG):
                    out_copy(a, h, b).wait_send()

    @pl.when(has_next)
    def _():
        for a in range(2):
            for h in range(HG):
                halo_copy(a, h, True).wait_send()
                halo_grad(False, a, h).wait_send()

    @pl.when(has_prev)
    def _():
        for a in range(2):
            for h in range(HG):
                halo_copy(a, h, False).wait_send()
                halo_grad(True, a, h).wait_send()


def store_kernel(a_in, b_in, c_in, d_in, sum_in, db_in, a, b, c, d, dsk, dsv, db, sems):
    copies = [
        pltpu.make_async_copy(src, dst, sems.at[i])
        for i, (src, dst) in enumerate(((a_in, a), (b_in, b), (c_in, c), (d_in, d)))
    ]
    for copy in copies:
        copy.start()
    rows = dsk.shape[1]
    both = sum_in[0].astype(F32)
    dsk[0] = both[:rows].astype(BF16)
    dsv[0] = both[rows:].astype(BF16)
    db[...] = db_in[...]
    for copy in copies:
        copy.wait()


def body(
    query_rows, key_rows, value_rows, summary_keys, summary_values, out_grad,
    rel_bias, pattern, block_view, summary_view,
):
    S = lax.axis_size("seq")
    D = lax.axis_size("dp")
    F = lax.axis_size("fsdp")
    T, W = query_rows.shape[1:]
    SR = summary_keys.shape[1]
    heads = W // HSIZE
    G = next(g for g in (4, 2, 1) if S % g == 0 and heads % g == 0)
    HG = heads // G
    WG = HG * HSIZE
    brows = -(-HG * NREL // 8) * 8
    table = lax.all_gather(rel_bias, "fsdp", axis=1, tiled=True) if F > 1 else rel_bias
    rows_ext = G * T + 2 * BLK
    vmem = pl.BlockSpec(memory_space=pltpu.VMEM)
    smem = pl.BlockSpec(memory_space=pltpu.SMEM)
    dma = pltpu.SemaphoreType.DMA
    anyspace = pl.BlockSpec(memory_space=pl.ANY)
    bias = jax.ShapeDtypeStruct(table.shape, F32)
    pair = jax.ShapeDtypeStruct((1, 2 * SR, W), BF16)
    summaries = jnp.concatenate([summary_keys, summary_values], axis=1)
    big = jax.ShapeDtypeStruct((1, T, W), BF16)
    small = jax.ShapeDtypeStruct((1, SR, W), BF16)
    results = pl.pallas_call(
        functools.partial(kernel, (S, D, G, T, W, HG, SR)),
        out_shape=(big, big, big, big, pair, bias),
        in_specs=[anyspace] * 5 + [smem] * 3 + [vmem],
        out_specs=[anyspace] * 4 + [vmem] * 2,
        scratch_shapes=[
            pltpu.VMEM((rows_ext, WG), BF16),
            pltpu.VMEM((rows_ext, WG), BF16),
            pltpu.VMEM((G * T, WG), BF16),
            pltpu.VMEM((G * T, WG), BF16),
            pltpu.VMEM((S, 2 * SR, WG), BF16),
            pltpu.VMEM((S * SR, WG), BF16),
            pltpu.VMEM((S * SR, WG), BF16),
            pltpu.VMEM((rows_ext, WG), F32),
            pltpu.VMEM((rows_ext, WG), F32),
            pltpu.VMEM((S * SR, WG), F32),
            pltpu.VMEM((S * SR, WG), F32),
            pltpu.VMEM((4, G * T, WG), BF16),
            pltpu.VMEM((HG, 4, BLK, HSIZE), BF16),
            pltpu.VMEM((HG, 4, BLK, HSIZE), BF16),
            pltpu.VMEM((S, 2 * SR, WG), BF16),
            pltpu.VMEM((S, 2 * SR, WG), BF16),
            pltpu.VMEM((brows, BLK), F32),
            pltpu.VMEM((S, brows, BLK), F32),
            pltpu.VMEM((D, G, brows, BLK), F32),
            dma((4, HG, G)), dma((4, HG, G)), dma((2, 2, HG)), dma((2, 2, HG)),
            dma((S,)), dma((S,)), dma((4, HG, G)), dma((4, HG, G)),
            dma((HG, 4)), dma((HG, 4)), dma((S,)), dma((S,)),
            dma((S,)), dma((S,)), dma((D,)), dma((D,)),
        ],
        compiler_params=pltpu.CompilerParams(
            collective_id=0, has_side_effects=True, vmem_limit_bytes=LIMIT
        ),
    )(
        query_rows, key_rows, value_rows, summaries, out_grad,
        table, pattern, block_view, summary_view,
    )
    whole = pl.BlockSpec((1, SR, W), lambda: (0, 0, 0))
    table_block = pl.BlockSpec(table.shape, lambda: (0, 0))
    results = pl.pallas_call(
        store_kernel,
        out_shape=(big, big, big, big, small, small, bias),
        in_specs=[anyspace] * 4 + [vmem] * 2,
        out_specs=[anyspace] * 4 + [whole, whole, table_block],
        scratch_shapes=[dma((4,))],
    )(*results)
    bias_grad = results[6]
    if F > 1:
        bias_total = lax.psum(bias_grad, "fsdp")
        part = table.shape[1] // F
        bias_grad = lax.dynamic_slice_in_dim(bias_total, lax.axis_index("fsdp") * part, part, 1)
    return (*results[:6], bias_grad)


def solution(mesh):
    rows = P("fsdp", "seq", "dp")
    placed = (
        rows, rows, rows, rows, rows, rows,
        P(None, "fsdp"), P("fsdp", None, None), P("fsdp", None), P("fsdp", None),
    )
    return jax.shard_map(
        body, mesh=mesh, in_specs=placed,
        out_specs=(rows, rows, rows, rows, rows, rows, P(None, "fsdp")),
        check_vma=False,
    )
```

```python
import functools
import math

import jax
import jax.numpy as jnp
from jax import lax
from jax.experimental import pallas as pl
from jax.experimental.pallas import tpu as pltpu
from jax.sharding import PartitionSpec as P

HSIZE = 128
BLK = 128
NVIEW = 96
NREL = 4
NEG_FILL = -1e30
LIMIT = 60 * 1024 * 1024
F32 = jnp.float32
BF16 = jnp.bfloat16


def cycle_class(view_a, view_b):
    distance = jnp.abs(view_a - view_b)
    distance = jnp.minimum(distance, NVIEW - distance)
    return (
        (distance >= 1).astype(jnp.int32)
        + (distance >= 2).astype(jnp.int32)
        + (distance >= 8).astype(jnp.int32)
    )


def dot_nt(a, b):
    return lax.dot_general(a, b, (((1,), (1,)), ((), ())), preferred_element_type=F32)


def dot_nn(a, b):
    return lax.dot_general(a, b, (((1,), (0,)), ((), ())), preferred_element_type=F32)


def dot_tn(a, b):
    return lax.dot_general(a, b, (((0,), (0,)), ((), ())), preferred_element_type=F32)


def kernel(
    sizes,
    q_ref, k_ref, v_ref, sum_out, do_ref, tab_ref, pat_ref, bv_ref, view_ref,
    att_ref, dq_ref, dk_ref, dv_ref, dsum_ref, db_ref,
    kx, vx, qg, dog, sum_in, ksm, vsm, dkx, dvx, dks, dvs,
    stage, halo_out, halo_in, rs_out, rs_in, b_out, b_in, x_in,
    in_send, in_recv, kv_send, kv_recv, sum_send, sum_recv, out_send, out_recv,
    hg_send, hg_recv, rs_send, rs_recv, b_send, b_recv, x_send, x_recv,
):
    S, D, G, T, W, HG, SR = sizes
    planes = S // G
    WG = HG * HSIZE
    H = G * HG
    blocks_dev = T // BLK
    nblk = G * blocks_dev
    total_blocks = planes * nblk
    scale = 1.0 / math.sqrt(HSIZE)
    brows = b_out.shape[0]

    s = lax.axis_index("seq")
    dp = lax.axis_index("dp")
    plane = s // G
    lane = lax.rem(s, G)
    first = plane * G

    def remote(src, dst, send, recv, target):
        return pltpu.make_async_remote_copy(
            src_ref=src, dst_ref=dst, send_sem=send, recv_sem=recv,
            device_id=target, device_id_type=pl.DeviceIdType.MESH,
        )

    def landed(dst, sem):
        pltpu.make_async_copy(dst, dst, sem).wait()

    barrier = pltpu.get_barrier_semaphore()
    for d in range(1, S):
        pl.semaphore_signal(
            barrier, inc=1, device_id={"seq": lax.rem(s + d, S)},
            device_id_type=pl.DeviceIdType.MESH,
        )
    for d in range(1, D):
        pl.semaphore_signal(
            barrier, inc=1, device_id={"dp": lax.rem(dp + d, D)},
            device_id_type=pl.DeviceIdType.MESH,
        )
    pl.semaphore_wait(barrier, S - 1 + D - 1)

    def cols(index):
        return pl.ds(pl.multiple_of(index * WG, WG), WG)

    def head_cols(index, h):
        return pl.ds(pl.multiple_of(index * WG + h * HSIZE, HSIZE), HSIZE)

    def rows_at(index, base):
        return pl.ds(pl.multiple_of(base + index * T, BLK), T)

    sends = []
    pairs = ((k_ref, kx, BLK), (v_ref, vx, BLK), (q_ref, qg, 0), (do_ref, dog, 0))

    def send_pairs(which, h):
        hc = pl.ds(h * HSIZE, HSIZE)
        for a in which:
            src, dst, base = pairs[a]
            for d in range(1, G):
                to = lax.rem(lane + d, G)
                copy = remote(
                    src.at[0, :, head_cols(to, h)], dst.at[rows_at(lane, base), hc],
                    in_send.at[a, h, d], in_recv.at[a, h, lane], {"seq": first + to},
                )
                copy.start()
                sends.append(copy)
            pltpu.make_async_copy(
                src.at[0, :, head_cols(lane, h)], dst.at[rows_at(lane, base), hc],
                in_recv.at[a, h, lane],
            ).start()

    send_pairs((0, 1), 0)
    for d in range(1, S):
        to = lax.rem(s + d, S)
        copy = remote(
            sum_out.at[0, :, cols(lax.rem(to, G))], sum_in.at[s],
            sum_send.at[d], sum_recv.at[s], {"seq": to},
        )
        copy.start()
        sends.append(copy)
    pltpu.make_async_copy(sum_out.at[0, :, cols(lane)], sum_in.at[s], sum_recv.at[s]).start()
    send_pairs((2, 3), 0)
    for h in range(1, HG):
        send_pairs((0, 1, 2, 3), h)

    dkx[...] = jnp.zeros_like(dkx)
    dvx[...] = jnp.zeros_like(dvx)
    dks[...] = jnp.zeros_like(dks)
    dvs[...] = jnp.zeros_like(dvs)

    has_prev = plane > 0
    has_next = plane < planes - 1
    top = (G * T, G * T + BLK)
    low = (BLK, 2 * BLK)
    last = (BLK + G * T, 2 * BLK + G * T)

    @pl.when(jnp.logical_not(has_prev))
    def _():
        for buf in (kx, vx):
            buf[0:BLK, :] = jnp.zeros((BLK, WG), BF16)

    @pl.when(jnp.logical_not(has_next))
    def _():
        for buf in (kx, vx):
            buf[last[0]:last[1], :] = jnp.zeros((BLK, WG), BF16)

    def halo_copy(a, h, forward):
        buf = (kx, vx)[a]
        hc = pl.ds(h * HSIZE, HSIZE)
        if forward:
            return remote(
                buf.at[pl.ds(top[0], BLK), hc], buf.at[pl.ds(0, BLK), hc],
                kv_send.at[0, a, h], kv_recv.at[0, a, h], {"seq": lax.rem(s + G, S)},
            )
        return remote(
            buf.at[pl.ds(low[0], BLK), hc], buf.at[pl.ds(last[0], BLK), hc],
            kv_send.at[1, a, h], kv_recv.at[1, a, h], {"seq": lax.rem(s + S - G, S)},
        )

    def take_keys(h):
        for a in range(2):
            for j in range(G):
                landed(
                    pairs[a][1].at[pl.ds(BLK + j * T, T), pl.ds(h * HSIZE, HSIZE)],
                    in_recv.at[a, h, j],
                )

        @pl.when(has_next)
        def _():
            for a in range(2):
                halo_copy(a, h, True).start()

        @pl.when(has_prev)
        def _():
            for a in range(2):
                halo_copy(a, h, False).start()

    def take_rest(h):
        hc = pl.ds(h * HSIZE, HSIZE)
        for a in (2, 3):
            for j in range(G):
                landed(pairs[a][1].at[pl.ds(j * T, T), hc], in_recv.at[a, h, j])

        @pl.when(has_prev)
        def _():
            for a in range(2):
                landed((kx, vx)[a].at[pl.ds(0, BLK), hc], kv_recv.at[0, a, h])

        @pl.when(has_next)
        def _():
            for a in range(2):
                landed((kx, vx)[a].at[pl.ds(last[0], BLK), hc], kv_recv.at[1, a, h])

    take_keys(0)
    for j in range(S):
        landed(sum_in.at[j], sum_recv.at[j])
    both = sum_in[...].astype(F32)
    ksm[...] = both[:, :SR, :].reshape(S * SR, WG).astype(BF16)
    vsm[...] = both[:, SR:, :].reshape(S * SR, WG).astype(BF16)
    view_rows = jnp.broadcast_to(view_ref[...].astype(F32), (BLK, S * SR)).T.astype(jnp.int32)

    bias_acc = [jnp.zeros((1, BLK), F32) for _ in range(HG * NREL)]

    def one_block(h, n):
        block = plane * nblk + n
        view = bv_ref[0, block]
        slot_class = []
        slot_open = []
        for j in range(3):
            near = jnp.clip(block + (j - 1), 0, total_blocks - 1)
            slot_class.append(cycle_class(view, bv_ref[0, near]))
            slot_open.append(pat_ref[0, block, j] >= 0)
        sum_class = cycle_class(view, view_rows)
        here = slice(n * BLK, (n + 1) * BLK)
        win = slice(n * BLK, (n + 3) * BLK)
        if True:
            hc = slice(h * HSIZE, (h + 1) * HSIZE)
            head = dp * H + lane * HG + h
            table = [tab_ref[c, head] for c in range(NREL)]
            q = qg[here, hc]
            do = dog[here, hc]
            kw = kx[win, hc]
            vw = vx[win, hc]
            ks = ksm[:, hc]
            vs = vsm[:, hc]
            raw = dot_nt(kw, q)
            scores = []
            for j in range(3):
                c = slot_class[j]
                b = jnp.where(
                    c >= 2, jnp.where(c == 3, table[3], table[2]),
                    jnp.where(c == 1, table[1], table[0]),
                )
                b = jnp.where(slot_open[j], b, NEG_FILL)
                scores.append(raw[j * BLK:(j + 1) * BLK] * scale + b)
            sum_bias = jnp.where(
                sum_class >= 2, jnp.where(sum_class == 3, table[3], table[2]),
                jnp.where(sum_class == 1, table[1], table[0]),
            )
            scores.append(dot_nt(ks, q) * scale + sum_bias)
            top_score = functools.reduce(
                jnp.maximum, [jnp.max(x, axis=0, keepdims=True) for x in scores]
            )
            lifted = [jnp.exp(x - top_score) for x in scores]
            total = sum(jnp.sum(x, axis=0, keepdims=True) for x in lifted)
            inverse = 1.0 / total
            weights = [x * inverse for x in lifted]
            dpw = dot_nt(vw, do)
            prob = [dpw[j * BLK:(j + 1) * BLK] for j in range(3)] + [dot_nt(vs, do)]
            delta = sum(jnp.sum(w * x, axis=0, keepdims=True) for w, x in zip(weights, prob))
            grads = [w * (x - delta) for w, x in zip(weights, prob)]
            w_win = jnp.concatenate([w.astype(BF16) for w in weights[:3]], axis=0)
            w_sum = weights[3].astype(BF16)
            g_win = jnp.concatenate([g.astype(BF16) for g in grads[:3]], axis=0)
            g_sum = grads[3].astype(BF16)
            stage[0, here, hc] = (dot_tn(w_win, vw) + dot_tn(w_sum, vs)).astype(BF16)
            stage[1, here, hc] = ((dot_tn(g_win, kw) + dot_tn(g_sum, ks)) * scale).astype(BF16)
            dkx[win, hc] += dot_nn(g_win, q)
            dvx[win, hc] += dot_nn(w_win, do)
            dks[:, hc] += dot_nn(g_sum, q)
            dvs[:, hc] += dot_nn(w_sum, do)
            slot_sums = [jnp.sum(g, axis=0, keepdims=True) for g in grads[:3]]
            for c in range(NREL):
                term = jnp.sum(jnp.where(sum_class == c, grads[3], 0.0), axis=0, keepdims=True)
                for j in range(3):
                    term = term + slot_sums[j] * jnp.where(slot_class[j] == c, 1.0, 0.0)
                bias_acc[h * NREL + c] = bias_acc[h * NREL + c] + term

    outs = (att_ref, dq_ref, dk_ref, dv_ref)

    def out_parts(a, h, b):
        return (
            stage.at[a, pl.ds(b * T, T), pl.ds(h * HSIZE, HSIZE)],
            outs[a].at[0, :, head_cols(lane, h)],
        )

    def out_copy(a, h, b):
        src, dst = out_parts(a, h, b)
        return remote(
            src, dst, out_send.at[a, h, b], out_recv.at[a, h, lane], {"seq": first + b}
        )

    def send_out(which, h, b):
        @pl.when(lane != b)
        def _():
            for a in which:
                out_copy(a, h, b).start()

        @pl.when(lane == b)
        def _():
            for a in which:
                src, dst = out_parts(a, h, b)
                pltpu.make_async_copy(src, dst, out_recv.at[a, h, lane]).start()

    def halo_grad(back, a, h):
        i = (0 if back else 2) + a
        return remote(
            halo_out.at[h, i], halo_in.at[h, i], hg_send.at[h, i], hg_recv.at[h, i],
            {"seq": lax.rem(s + (S - G if back else G), S)},
        )

    def finish(h, b):
        span = slice(BLK + b * T, BLK + (b + 1) * T)
        hc = slice(h * HSIZE, (h + 1) * HSIZE)
        stage[2, b * T:(b + 1) * T, hc] = (dkx[span, hc] * scale).astype(BF16)
        stage[3, b * T:(b + 1) * T, hc] = dvx[span, hc].astype(BF16)
        send_out((2, 3), h, b)

    def finish_ends(h):
        hc = slice(h * HSIZE, (h + 1) * HSIZE)

        @pl.when(has_prev)
        def _():
            for a, buf in enumerate((dkx, dvx)):
                landed(halo_in.at[h, 2 + a], hg_recv.at[h, 2 + a])
                buf[low[0]:low[1], hc] += halo_in[h, 2 + a].astype(F32)

        @pl.when(has_next)
        def _():
            for a, buf in enumerate((dkx, dvx)):
                landed(halo_in.at[h, a], hg_recv.at[h, a])
                buf[top[0]:top[1], hc] += halo_in[h, a].astype(F32)

        for b in sorted({0, G - 1}):
            finish(h, b)

    order = list(dict.fromkeys([0, G - 1] + list(range(1, G - 1))))
    half = len(order) // 2
    for h in range(HG):
        hc = slice(h * HSIZE, (h + 1) * HSIZE)
        take_rest(h)
        for step, b in enumerate(order):
            if step == half:
                if h + 1 < HG:
                    take_keys(h + 1)
                if h > 0:
                    finish_ends(h - 1)
            for i in range(blocks_dev):
                one_block(h, b * blocks_dev + i)
            send_out((0, 1), h, b)
            if b == 0:
                halo_out[h, 0] = dkx[0:BLK, hc].astype(BF16)
                halo_out[h, 1] = dvx[0:BLK, hc].astype(BF16)

                @pl.when(has_prev)
                def _():
                    for a in range(2):
                        halo_grad(True, a, h).start()
            if b == G - 1:
                halo_out[h, 2] = dkx[last[0]:last[1], hc].astype(BF16)
                halo_out[h, 3] = dvx[last[0]:last[1], hc].astype(BF16)

                @pl.when(has_next)
                def _():
                    for a in range(2):
                        halo_grad(False, a, h).start()
        for b in range(1, G - 1):
            finish(h, b)

    packed = jnp.concatenate(
        [(dks[...] * scale).reshape(S, SR, WG), dvs[...].reshape(S, SR, WG)], axis=1
    )
    rs_out[...] = packed.astype(BF16)
    pad = brows - HG * NREL
    b_out[...] = jnp.concatenate(
        bias_acc + ([jnp.zeros((pad, BLK), F32)] if pad else []), axis=0
    )
    for d in range(1, S):
        to = lax.rem(s + d, S)
        copy = remote(b_out, b_in.at[s], b_send.at[d], b_recv.at[s], {"seq": to})
        copy.start()
        sends.append(copy)
        copy = remote(rs_out.at[to], rs_in.at[s], rs_send.at[d], rs_recv.at[s], {"seq": to})
        copy.start()
        sends.append(copy)
    pltpu.make_async_copy(b_out, b_in.at[s], b_recv.at[s]).start()
    pltpu.make_async_copy(rs_out.at[s], rs_in.at[s], rs_recv.at[s]).start()

    finish_ends(HG - 1)

    for j in range(S):
        landed(b_in.at[j], b_recv.at[j])
    x_in[dp] = jnp.sum(b_in[...].reshape(planes, G, brows, BLK), axis=0)
    for d in range(1, D):
        copy = remote(
            x_in.at[dp], x_in.at[dp], x_send.at[d], x_recv.at[dp], {"dp": lax.rem(dp + d, D)}
        )
        copy.start()
        sends.append(copy)

    for j in range(S):
        landed(rs_in.at[j], rs_recv.at[j])
    terms = jnp.sum(rs_in[...].astype(F32).reshape(planes, G, 2 * SR, WG), axis=0)
    for g in range(G):
        gc = slice(g * WG, (g + 1) * WG)
        dsum_ref[0, :, gc] = terms[g].astype(BF16)

    for d in range(1, D):
        who = lax.rem(dp + d, D)
        landed(x_in.at[who], x_recv.at[who])
    lanes = lax.broadcasted_iota(jnp.int32, db_ref.shape, 1)
    result = jnp.zeros(db_ref.shape, F32)
    for e in range(D):
        for g in range(G):
            column = jnp.sum(x_in[e, g], axis=1, keepdims=True)
            for h in range(HG):
                at = e * H + g * HG + h
                result = jnp.where(lanes == at, column[h * NREL:(h + 1) * NREL], result)
    db_ref[...] = result

    for a in range(4):
        for h in range(HG):
            for j in range(G):
                landed(
                    outs[a].at[0, :, pl.ds(j * WG + h * HSIZE, HSIZE)], out_recv.at[a, h, j]
                )

    for copy in sends:
        copy.wait_send()
    for b in range(G):
        @pl.when(lane != b)
        def _():
            for a in range(4):
                for h in range(HG):
                    out_copy(a, h, b).wait_send()

    @pl.when(has_next)
    def _():
        for a in range(2):
            for h in range(HG):
                halo_copy(a, h, True).wait_send()
                halo_grad(False, a, h).wait_send()

    @pl.when(has_prev)
    def _():
        for a in range(2):
            for h in range(HG):
                halo_copy(a, h, False).wait_send()
                halo_grad(True, a, h).wait_send()


def store_kernel(
    a_in, b_in, c_in, d_in, sum_in, db_in, a, b, c, d, dsk, dsv, db, hold, in_sems, out_sems
):
    sources = (a_in, b_in, c_in, d_in)
    loads = [
        pltpu.make_async_copy(src, hold.at[i], in_sems.at[i]) for i, src in enumerate(sources)
    ]
    copies = [
        pltpu.make_async_copy(hold.at[i], dst, out_sems.at[i])
        for i, dst in enumerate((a, b, c, d))
    ]
    for load in loads:
        load.start()
    rows = dsk.shape[1]
    both = sum_in[0].astype(F32)
    dsk[0] = both[:rows].astype(BF16)
    dsv[0] = both[rows:].astype(BF16)
    db[...] = db_in[...]
    for load, copy in zip(loads, copies):
        load.wait()
        copy.start()
    for copy in copies:
        copy.wait()


def body(
    query_rows, key_rows, value_rows, summary_keys, summary_values, out_grad,
    rel_bias, pattern, block_view, summary_view,
):
    S = lax.axis_size("seq")
    D = lax.axis_size("dp")
    F = lax.axis_size("fsdp")
    T, W = query_rows.shape[1:]
    SR = summary_keys.shape[1]
    heads = W // HSIZE
    G = next(g for g in (4, 2, 1) if S % g == 0 and heads % g == 0)
    HG = heads // G
    WG = HG * HSIZE
    brows = -(-HG * NREL // 8) * 8
    table = lax.all_gather(rel_bias, "fsdp", axis=1, tiled=True) if F > 1 else rel_bias
    rows_ext = G * T + 2 * BLK
    vmem = pl.BlockSpec(memory_space=pltpu.VMEM)
    smem = pl.BlockSpec(memory_space=pltpu.SMEM)
    dma = pltpu.SemaphoreType.DMA
    anyspace = pl.BlockSpec(memory_space=pl.ANY)
    bias = jax.ShapeDtypeStruct(table.shape, F32)
    pair = jax.ShapeDtypeStruct((1, 2 * SR, W), BF16)
    summaries = jnp.concatenate([summary_keys, summary_values], axis=1)
    big = jax.ShapeDtypeStruct((1, T, W), BF16)
    small = jax.ShapeDtypeStruct((1, SR, W), BF16)
    results = pl.pallas_call(
        functools.partial(kernel, (S, D, G, T, W, HG, SR)),
        out_shape=(big, big, big, big, pair, bias),
        in_specs=[anyspace] * 5 + [smem] * 3 + [vmem],
        out_specs=[anyspace] * 4 + [vmem] * 2,
        scratch_shapes=[
            pltpu.VMEM((rows_ext, WG), BF16),
            pltpu.VMEM((rows_ext, WG), BF16),
            pltpu.VMEM((G * T, WG), BF16),
            pltpu.VMEM((G * T, WG), BF16),
            pltpu.VMEM((S, 2 * SR, WG), BF16),
            pltpu.VMEM((S * SR, WG), BF16),
            pltpu.VMEM((S * SR, WG), BF16),
            pltpu.VMEM((rows_ext, WG), F32),
            pltpu.VMEM((rows_ext, WG), F32),
            pltpu.VMEM((S * SR, WG), F32),
            pltpu.VMEM((S * SR, WG), F32),
            pltpu.VMEM((4, G * T, WG), BF16),
            pltpu.VMEM((HG, 4, BLK, HSIZE), BF16),
            pltpu.VMEM((HG, 4, BLK, HSIZE), BF16),
            pltpu.VMEM((S, 2 * SR, WG), BF16),
            pltpu.VMEM((S, 2 * SR, WG), BF16),
            pltpu.VMEM((brows, BLK), F32),
            pltpu.VMEM((S, brows, BLK), F32),
            pltpu.VMEM((D, G, brows, BLK), F32),
            dma((4, HG, G)), dma((4, HG, G)), dma((2, 2, HG)), dma((2, 2, HG)),
            dma((S,)), dma((S,)), dma((4, HG, G)), dma((4, HG, G)),
            dma((HG, 4)), dma((HG, 4)), dma((S,)), dma((S,)),
            dma((S,)), dma((S,)), dma((D,)), dma((D,)),
        ],
        compiler_params=pltpu.CompilerParams(
            collective_id=0, has_side_effects=True, vmem_limit_bytes=LIMIT
        ),
    )(
        query_rows, key_rows, value_rows, summaries, out_grad,
        table, pattern, block_view, summary_view,
    )
    whole = pl.BlockSpec((1, SR, W), lambda: (0, 0, 0))
    table_block = pl.BlockSpec(table.shape, lambda: (0, 0))
    results = pl.pallas_call(
        store_kernel,
        out_shape=(big, big, big, big, small, small, bias),
        in_specs=[anyspace] * 4 + [vmem] * 2,
        out_specs=[anyspace] * 4 + [whole, whole, table_block],
        scratch_shapes=[pltpu.VMEM((4, 1, T, W), BF16), dma((4,)), dma((4,))],
    )(*results)
    bias_grad = results[6]
    if F > 1:
        bias_total = lax.psum(bias_grad, "fsdp")
        part = table.shape[1] // F
        bias_grad = lax.dynamic_slice_in_dim(bias_total, lax.axis_index("fsdp") * part, part, 1)
    return (*results[:6], bias_grad)


def solution(mesh):
    rows = P("fsdp", "seq", "dp")
    placed = (
        rows, rows, rows, rows, rows, rows,
        P(None, "fsdp"), P("fsdp", None, None), P("fsdp", None), P("fsdp", None),
    )
    return jax.shard_map(
        body, mesh=mesh, in_specs=placed,
        out_specs=(rows, rows, rows, rows, rows, rows, P(None, "fsdp")),
        check_vma=False,
    )
```

```python
import functools
import math

import jax
import jax.numpy as jnp
from jax import lax
from jax.experimental import pallas as pl
from jax.experimental.pallas import tpu as pltpu
from jax.sharding import PartitionSpec as P

HSIZE = 128
BLK = 128
NVIEW = 96
NREL = 4
NEG_FILL = -1e30
LIMIT = 60 * 1024 * 1024
F32 = jnp.float32
BF16 = jnp.bfloat16


def cycle_class(view_a, view_b):
    distance = jnp.abs(view_a - view_b)
    distance = jnp.minimum(distance, NVIEW - distance)
    return (
        (distance >= 1).astype(jnp.int32)
        + (distance >= 2).astype(jnp.int32)
        + (distance >= 8).astype(jnp.int32)
    )


def dot_nt(a, b):
    return lax.dot_general(a, b, (((1,), (1,)), ((), ())), preferred_element_type=F32)


def dot_nn(a, b):
    return lax.dot_general(a, b, (((1,), (0,)), ((), ())), preferred_element_type=F32)


def dot_tn(a, b):
    return lax.dot_general(a, b, (((0,), (0,)), ((), ())), preferred_element_type=F32)


def kernel(
    sizes,
    q_ref, k_ref, v_ref, sum_out, do_ref, tab_ref, pat_ref, bv_ref, view_ref,
    att_ref, dq_ref, dk_ref, dv_ref, dsum_ref, db_ref,
    kx, vx, qg, dog, sum_in, ksm, vsm, dkx, dvx, dks, dvs,
    stage, halo_out, halo_in, rs_out, rs_in, b_out, b_in, x_in,
    in_send, in_recv, kv_send, kv_recv, sum_send, sum_recv, out_send, out_recv,
    hg_send, hg_recv, rs_send, rs_recv, b_send, b_recv, x_send, x_recv,
):
    S, D, G, T, W, HG, SR = sizes
    planes = S // G
    WG = HG * HSIZE
    H = G * HG
    blocks_dev = T // BLK
    nblk = G * blocks_dev
    total_blocks = planes * nblk
    scale = 1.0 / math.sqrt(HSIZE)
    brows = b_out.shape[0]

    s = lax.axis_index("seq")
    dp = lax.axis_index("dp")
    plane = s // G
    lane = lax.rem(s, G)
    first = plane * G

    def remote(src, dst, send, recv, target):
        return pltpu.make_async_remote_copy(
            src_ref=src, dst_ref=dst, send_sem=send, recv_sem=recv,
            device_id=target, device_id_type=pl.DeviceIdType.MESH,
        )

    def landed(dst, sem):
        pltpu.make_async_copy(dst, dst, sem).wait()

    barrier = pltpu.get_barrier_semaphore()
    for d in range(1, S):
        pl.semaphore_signal(
            barrier, inc=1, device_id={"seq": lax.rem(s + d, S)},
            device_id_type=pl.DeviceIdType.MESH,
        )
    for d in range(1, D):
        pl.semaphore_signal(
            barrier, inc=1, device_id={"dp": lax.rem(dp + d, D)},
            device_id_type=pl.DeviceIdType.MESH,
        )
    pl.semaphore_wait(barrier, S - 1 + D - 1)

    def cols(index):
        return pl.ds(pl.multiple_of(index * WG, WG), WG)

    def head_cols(index, h):
        return pl.ds(pl.multiple_of(index * WG + h * HSIZE, HSIZE), HSIZE)

    def rows_at(index, base):
        return pl.ds(pl.multiple_of(base + index * T, BLK), T)

    sends = []
    pairs = ((k_ref, kx, BLK), (v_ref, vx, BLK), (q_ref, qg, 0), (do_ref, dog, 0))

    def send_pairs(which, h):
        hc = pl.ds(h * HSIZE, HSIZE)
        for a in which:
            src, dst, base = pairs[a]
            for d in range(1, G):
                to = lax.rem(lane + d, G)
                copy = remote(
                    src.at[0, :, head_cols(to, h)], dst.at[rows_at(lane, base), hc],
                    in_send.at[a, h, d], in_recv.at[a, h, lane], {"seq": first + to},
                )
                copy.start()
                sends.append(copy)
            pltpu.make_async_copy(
                src.at[0, :, head_cols(lane, h)], dst.at[rows_at(lane, base), hc],
                in_recv.at[a, h, lane],
            ).start()

    send_pairs((0, 1), 0)
    for d in range(1, S):
        to = lax.rem(s + d, S)
        copy = remote(
            sum_out.at[0, :, cols(lax.rem(to, G))], sum_in.at[s],
            sum_send.at[d], sum_recv.at[s], {"seq": to},
        )
        copy.start()
        sends.append(copy)
    pltpu.make_async_copy(sum_out.at[0, :, cols(lane)], sum_in.at[s], sum_recv.at[s]).start()
    send_pairs((2, 3), 0)
    for h in range(1, HG):
        send_pairs((0, 1, 2, 3), h)

    dkx[...] = jnp.zeros_like(dkx)
    dvx[...] = jnp.zeros_like(dvx)
    dks[...] = jnp.zeros_like(dks)
    dvs[...] = jnp.zeros_like(dvs)

    has_prev = plane > 0
    has_next = plane < planes - 1
    top = (G * T, G * T + BLK)
    low = (BLK, 2 * BLK)
    last = (BLK + G * T, 2 * BLK + G * T)

    @pl.when(jnp.logical_not(has_prev))
    def _():
        for buf in (kx, vx):
            buf[0:BLK, :] = jnp.zeros((BLK, WG), BF16)

    @pl.when(jnp.logical_not(has_next))
    def _():
        for buf in (kx, vx):
            buf[last[0]:last[1], :] = jnp.zeros((BLK, WG), BF16)

    def halo_copy(a, h, forward):
        buf = (kx, vx)[a]
        hc = pl.ds(h * HSIZE, HSIZE)
        if forward:
            return remote(
                buf.at[pl.ds(top[0], BLK), hc], buf.at[pl.ds(0, BLK), hc],
                kv_send.at[0, a, h], kv_recv.at[0, a, h], {"seq": lax.rem(s + G, S)},
            )
        return remote(
            buf.at[pl.ds(low[0], BLK), hc], buf.at[pl.ds(last[0], BLK), hc],
            kv_send.at[1, a, h], kv_recv.at[1, a, h], {"seq": lax.rem(s + S - G, S)},
        )

    def take_keys(h):
        for a in range(2):
            for j in range(G):
                landed(
                    pairs[a][1].at[pl.ds(BLK + j * T, T), pl.ds(h * HSIZE, HSIZE)],
                    in_recv.at[a, h, j],
                )

        @pl.when(has_next)
        def _():
            for a in range(2):
                halo_copy(a, h, True).start()

        @pl.when(has_prev)
        def _():
            for a in range(2):
                halo_copy(a, h, False).start()

    def take_rest(h):
        hc = pl.ds(h * HSIZE, HSIZE)
        for a in (2, 3):
            for j in range(G):
                landed(pairs[a][1].at[pl.ds(j * T, T), hc], in_recv.at[a, h, j])

        @pl.when(has_prev)
        def _():
            for a in range(2):
                landed((kx, vx)[a].at[pl.ds(0, BLK), hc], kv_recv.at[0, a, h])

        @pl.when(has_next)
        def _():
            for a in range(2):
                landed((kx, vx)[a].at[pl.ds(last[0], BLK), hc], kv_recv.at[1, a, h])

    take_keys(0)
    for j in range(S):
        landed(sum_in.at[j], sum_recv.at[j])
    both = sum_in[...].astype(F32)
    ksm[...] = both[:, :SR, :].reshape(S * SR, WG).astype(BF16)
    vsm[...] = both[:, SR:, :].reshape(S * SR, WG).astype(BF16)
    view_rows = jnp.broadcast_to(view_ref[...].astype(F32), (BLK, S * SR)).T.astype(jnp.int32)

    bias_acc = [jnp.zeros((1, BLK), F32) for _ in range(HG * NREL)]

    def one_block(h, n):
        block = plane * nblk + n
        view = bv_ref[0, block]
        slot_class = []
        slot_open = []
        for j in range(3):
            near = jnp.clip(block + (j - 1), 0, total_blocks - 1)
            slot_class.append(cycle_class(view, bv_ref[0, near]))
            slot_open.append(pat_ref[0, block, j] >= 0)
        sum_class = cycle_class(view, view_rows)
        here = slice(n * BLK, (n + 1) * BLK)
        win = slice(n * BLK, (n + 3) * BLK)
        if True:
            hc = slice(h * HSIZE, (h + 1) * HSIZE)
            head = dp * H + lane * HG + h
            table = [tab_ref[c, head] for c in range(NREL)]
            q = qg[here, hc]
            do = dog[here, hc]
            kw = kx[win, hc]
            vw = vx[win, hc]
            ks = ksm[:, hc]
            vs = vsm[:, hc]
            raw = dot_nt(kw, q)
            scores = []
            for j in range(3):
                c = slot_class[j]
                b = jnp.where(
                    c >= 2, jnp.where(c == 3, table[3], table[2]),
                    jnp.where(c == 1, table[1], table[0]),
                )
                b = jnp.where(slot_open[j], b, NEG_FILL)
                scores.append(raw[j * BLK:(j + 1) * BLK] * scale + b)
            sum_bias = jnp.where(
                sum_class >= 2, jnp.where(sum_class == 3, table[3], table[2]),
                jnp.where(sum_class == 1, table[1], table[0]),
            )
            scores.append(dot_nt(ks, q) * scale + sum_bias)
            top_score = functools.reduce(
                jnp.maximum, [jnp.max(x, axis=0, keepdims=True) for x in scores]
            )
            lifted = [jnp.exp(x - top_score) for x in scores]
            total = sum(jnp.sum(x, axis=0, keepdims=True) for x in lifted)
            inverse = 1.0 / total
            weights = [x * inverse for x in lifted]
            dpw = dot_nt(vw, do)
            prob = [dpw[j * BLK:(j + 1) * BLK] for j in range(3)] + [dot_nt(vs, do)]
            delta = sum(jnp.sum(w * x, axis=0, keepdims=True) for w, x in zip(weights, prob))
            grads = [w * (x - delta) for w, x in zip(weights, prob)]
            w_win = jnp.concatenate([w.astype(BF16) for w in weights[:3]], axis=0)
            w_sum = weights[3].astype(BF16)
            g_win = jnp.concatenate([g.astype(BF16) for g in grads[:3]], axis=0)
            g_sum = grads[3].astype(BF16)
            stage[0, here, hc] = (dot_tn(w_win, vw) + dot_tn(w_sum, vs)).astype(BF16)
            stage[1, here, hc] = ((dot_tn(g_win, kw) + dot_tn(g_sum, ks)) * scale).astype(BF16)
            dkx[win, hc] += dot_nn(g_win, q)
            dvx[win, hc] += dot_nn(w_win, do)
            dks[:, hc] += dot_nn(g_sum, q)
            dvs[:, hc] += dot_nn(w_sum, do)
            slot_sums = [jnp.sum(g, axis=0, keepdims=True) for g in grads[:3]]
            for c in range(NREL):
                term = jnp.sum(jnp.where(sum_class == c, grads[3], 0.0), axis=0, keepdims=True)
                for j in range(3):
                    term = term + slot_sums[j] * jnp.where(slot_class[j] == c, 1.0, 0.0)
                bias_acc[h * NREL + c] = bias_acc[h * NREL + c] + term

    outs = (att_ref, dq_ref, dk_ref, dv_ref)

    def out_parts(a, h, b):
        return (
            stage.at[a, pl.ds(b * T, T), pl.ds(h * HSIZE, HSIZE)],
            outs[a].at[0, :, head_cols(lane, h)],
        )

    def out_copy(a, h, b):
        src, dst = out_parts(a, h, b)
        return remote(
            src, dst, out_send.at[a, h, b], out_recv.at[a, h, lane], {"seq": first + b}
        )

    def send_out(which, h, b):
        @pl.when(lane != b)
        def _():
            for a in which:
                out_copy(a, h, b).start()

        @pl.when(lane == b)
        def _():
            for a in which:
                src, dst = out_parts(a, h, b)
                pltpu.make_async_copy(src, dst, out_recv.at[a, h, lane]).start()

    def halo_grad(back, a, h):
        i = (0 if back else 2) + a
        return remote(
            halo_out.at[h, i], halo_in.at[h, i], hg_send.at[h, i], hg_recv.at[h, i],
            {"seq": lax.rem(s + (S - G if back else G), S)},
        )

    def finish(h, b):
        span = slice(BLK + b * T, BLK + (b + 1) * T)
        hc = slice(h * HSIZE, (h + 1) * HSIZE)
        stage[2, b * T:(b + 1) * T, hc] = (dkx[span, hc] * scale).astype(BF16)
        stage[3, b * T:(b + 1) * T, hc] = dvx[span, hc].astype(BF16)
        send_out((2, 3), h, b)

    def finish_ends(h):
        hc = slice(h * HSIZE, (h + 1) * HSIZE)

        @pl.when(has_prev)
        def _():
            for a, buf in enumerate((dkx, dvx)):
                landed(halo_in.at[h, 2 + a], hg_recv.at[h, 2 + a])
                buf[low[0]:low[1], hc] += halo_in[h, 2 + a].astype(F32)

        @pl.when(has_next)
        def _():
            for a, buf in enumerate((dkx, dvx)):
                landed(halo_in.at[h, a], hg_recv.at[h, a])
                buf[top[0]:top[1], hc] += halo_in[h, a].astype(F32)

        for b in sorted({0, G - 1}):
            finish(h, b)

    order = list(dict.fromkeys([0, G - 1] + list(range(1, G - 1))))
    half = len(order) // 2
    for h in range(HG):
        hc = slice(h * HSIZE, (h + 1) * HSIZE)
        take_rest(h)
        for step, b in enumerate(order):
            if step == half:
                if h + 1 < HG:
                    take_keys(h + 1)
                if h > 0:
                    finish_ends(h - 1)
            for i in range(blocks_dev):
                one_block(h, b * blocks_dev + i)
            send_out((0, 1), h, b)
            if b == 0:
                halo_out[h, 0] = dkx[0:BLK, hc].astype(BF16)
                halo_out[h, 1] = dvx[0:BLK, hc].astype(BF16)

                @pl.when(has_prev)
                def _():
                    for a in range(2):
                        halo_grad(True, a, h).start()
            if b == G - 1:
                halo_out[h, 2] = dkx[last[0]:last[1], hc].astype(BF16)
                halo_out[h, 3] = dvx[last[0]:last[1], hc].astype(BF16)

                @pl.when(has_next)
                def _():
                    for a in range(2):
                        halo_grad(False, a, h).start()
        for b in range(1, G - 1):
            finish(h, b)

    packed = jnp.concatenate(
        [(dks[...] * scale).reshape(S, SR, WG), dvs[...].reshape(S, SR, WG)], axis=1
    )
    rs_out[...] = packed.astype(BF16)
    pad = brows - HG * NREL
    b_out[...] = jnp.concatenate(
        bias_acc + ([jnp.zeros((pad, BLK), F32)] if pad else []), axis=0
    )
    finish_ends(HG - 1)

    for d in range(1, S):
        to = lax.rem(s + d, S)
        copy = remote(b_out, b_in.at[s], b_send.at[d], b_recv.at[s], {"seq": to})
        copy.start()
        sends.append(copy)
        copy = remote(rs_out.at[to], rs_in.at[s], rs_send.at[d], rs_recv.at[s], {"seq": to})
        copy.start()
        sends.append(copy)
    pltpu.make_async_copy(b_out, b_in.at[s], b_recv.at[s]).start()
    pltpu.make_async_copy(rs_out.at[s], rs_in.at[s], rs_recv.at[s]).start()

    for j in range(S):
        landed(b_in.at[j], b_recv.at[j])
    x_in[dp] = jnp.sum(b_in[...].reshape(planes, G, brows, BLK), axis=0)
    for d in range(1, D):
        copy = remote(
            x_in.at[dp], x_in.at[dp], x_send.at[d], x_recv.at[dp], {"dp": lax.rem(dp + d, D)}
        )
        copy.start()
        sends.append(copy)

    for j in range(S):
        landed(rs_in.at[j], rs_recv.at[j])
    terms = jnp.sum(rs_in[...].astype(F32).reshape(planes, G, 2 * SR, WG), axis=0)
    for g in range(G):
        gc = slice(g * WG, (g + 1) * WG)
        dsum_ref[0, :, gc] = terms[g].astype(BF16)

    for d in range(1, D):
        who = lax.rem(dp + d, D)
        landed(x_in.at[who], x_recv.at[who])
    lanes = lax.broadcasted_iota(jnp.int32, db_ref.shape, 1)
    result = jnp.zeros(db_ref.shape, F32)
    for e in range(D):
        for g in range(G):
            column = jnp.sum(x_in[e, g], axis=1, keepdims=True)
            for h in range(HG):
                at = e * H + g * HG + h
                result = jnp.where(lanes == at, column[h * NREL:(h + 1) * NREL], result)
    db_ref[...] = result

    for a in range(4):
        for h in range(HG):
            for j in range(G):
                landed(
                    outs[a].at[0, :, pl.ds(j * WG + h * HSIZE, HSIZE)], out_recv.at[a, h, j]
                )

    for copy in sends:
        copy.wait_send()
    for b in range(G):
        @pl.when(lane != b)
        def _():
            for a in range(4):
                for h in range(HG):
                    out_copy(a, h, b).wait_send()

    @pl.when(has_next)
    def _():
        for a in range(2):
            for h in range(HG):
                halo_copy(a, h, True).wait_send()
                halo_grad(False, a, h).wait_send()

    @pl.when(has_prev)
    def _():
        for a in range(2):
            for h in range(HG):
                halo_copy(a, h, False).wait_send()
                halo_grad(True, a, h).wait_send()


def store_kernel(
    a_in, b_in, c_in, d_in, sum_in, db_in, a, b, c, d, dsk, dsv, db, hold, in_sems, out_sems
):
    sources = (a_in, b_in, c_in, d_in)
    loads = [
        pltpu.make_async_copy(src, hold.at[i], in_sems.at[i]) for i, src in enumerate(sources)
    ]
    copies = [
        pltpu.make_async_copy(hold.at[i], dst, out_sems.at[i])
        for i, dst in enumerate((a, b, c, d))
    ]
    for load in loads:
        load.start()
    rows = dsk.shape[1]
    both = sum_in[0].astype(F32)
    dsk[0] = both[:rows].astype(BF16)
    dsv[0] = both[rows:].astype(BF16)
    db[...] = db_in[...]
    for load, copy in zip(loads, copies):
        load.wait()
        copy.start()
    for copy in copies:
        copy.wait()


def body(
    query_rows, key_rows, value_rows, summary_keys, summary_values, out_grad,
    rel_bias, pattern, block_view, summary_view,
):
    S = lax.axis_size("seq")
    D = lax.axis_size("dp")
    F = lax.axis_size("fsdp")
    T, W = query_rows.shape[1:]
    SR = summary_keys.shape[1]
    heads = W // HSIZE
    G = next(g for g in (4, 2, 1) if S % g == 0 and heads % g == 0)
    HG = heads // G
    WG = HG * HSIZE
    brows = -(-HG * NREL // 8) * 8
    table = lax.all_gather(rel_bias, "fsdp", axis=1, tiled=True) if F > 1 else rel_bias
    rows_ext = G * T + 2 * BLK
    vmem = pl.BlockSpec(memory_space=pltpu.VMEM)
    smem = pl.BlockSpec(memory_space=pltpu.SMEM)
    dma = pltpu.SemaphoreType.DMA
    anyspace = pl.BlockSpec(memory_space=pl.ANY)
    bias = jax.ShapeDtypeStruct(table.shape, F32)
    pair = jax.ShapeDtypeStruct((1, 2 * SR, W), BF16)
    summaries = jnp.concatenate([summary_keys, summary_values], axis=1)
    big = jax.ShapeDtypeStruct((1, T, W), BF16)
    small = jax.ShapeDtypeStruct((1, SR, W), BF16)
    results = pl.pallas_call(
        functools.partial(kernel, (S, D, G, T, W, HG, SR)),
        out_shape=(big, big, big, big, pair, bias),
        in_specs=[anyspace] * 5 + [smem] * 3 + [vmem],
        out_specs=[anyspace] * 4 + [vmem] * 2,
        scratch_shapes=[
            pltpu.VMEM((rows_ext, WG), BF16),
            pltpu.VMEM((rows_ext, WG), BF16),
            pltpu.VMEM((G * T, WG), BF16),
            pltpu.VMEM((G * T, WG), BF16),
            pltpu.VMEM((S, 2 * SR, WG), BF16),
            pltpu.VMEM((S * SR, WG), BF16),
            pltpu.VMEM((S * SR, WG), BF16),
            pltpu.VMEM((rows_ext, WG), F32),
            pltpu.VMEM((rows_ext, WG), F32),
            pltpu.VMEM((S * SR, WG), F32),
            pltpu.VMEM((S * SR, WG), F32),
            pltpu.VMEM((4, G * T, WG), BF16),
            pltpu.VMEM((HG, 4, BLK, HSIZE), BF16),
            pltpu.VMEM((HG, 4, BLK, HSIZE), BF16),
            pltpu.VMEM((S, 2 * SR, WG), BF16),
            pltpu.VMEM((S, 2 * SR, WG), BF16),
            pltpu.VMEM((brows, BLK), F32),
            pltpu.VMEM((S, brows, BLK), F32),
            pltpu.VMEM((D, G, brows, BLK), F32),
            dma((4, HG, G)), dma((4, HG, G)), dma((2, 2, HG)), dma((2, 2, HG)),
            dma((S,)), dma((S,)), dma((4, HG, G)), dma((4, HG, G)),
            dma((HG, 4)), dma((HG, 4)), dma((S,)), dma((S,)),
            dma((S,)), dma((S,)), dma((D,)), dma((D,)),
        ],
        compiler_params=pltpu.CompilerParams(
            collective_id=0, has_side_effects=True, vmem_limit_bytes=LIMIT
        ),
    )(
        query_rows, key_rows, value_rows, summaries, out_grad,
        table, pattern, block_view, summary_view,
    )
    whole = pl.BlockSpec((1, SR, W), lambda: (0, 0, 0))
    table_block = pl.BlockSpec(table.shape, lambda: (0, 0))
    results = pl.pallas_call(
        store_kernel,
        out_shape=(big, big, big, big, small, small, bias),
        in_specs=[anyspace] * 4 + [vmem] * 2,
        out_specs=[anyspace] * 4 + [whole, whole, table_block],
        scratch_shapes=[pltpu.VMEM((4, 1, T, W), BF16), dma((4,)), dma((4,))],
    )(*results)
    bias_grad = results[6]
    if F > 1:
        bias_total = lax.psum(bias_grad, "fsdp")
        part = table.shape[1] // F
        bias_grad = lax.dynamic_slice_in_dim(bias_total, lax.axis_index("fsdp") * part, part, 1)
    return (*results[:6], bias_grad)


def solution(mesh):
    rows = P("fsdp", "seq", "dp")
    placed = (
        rows, rows, rows, rows, rows, rows,
        P(None, "fsdp"), P("fsdp", None, None), P("fsdp", None), P("fsdp", None),
    )
    return jax.shard_map(
        body, mesh=mesh, in_specs=placed,
        out_specs=(rows, rows, rows, rows, rows, rows, P(None, "fsdp")),
        check_vma=False,
    )
```
